32 devices in a mesh: groups: 1, tile: 16 (over z, y, x), col: 2 (over core).
Axes of the slice: x: 2, y: 2, z: 4, core: 2. Of those that a mesh axis runs over, the one named last changes fastest.
Arguments:
- zonal_velocity: float32 [50, 512, 256], P(None, ('groups', 'tile'), 'col'), may hold values from -4 to 4
- meridional_velocity: float32 [50, 512, 256], P(None, ('groups', 'tile'), 'col'), may hold values from -4 to 4
- surface_height: float32 [512, 256], P(('groups', 'tile'), 'col'), may hold values from -3 to 3
- thickness: float32 [50], replicated, may hold values from 0.5 to 2
- mixing: float32 [50], replicated, may hold values from 0.02 to 0.2
- ocean_wet: int32 [512, 256], P(('groups', 'tile'), 'col'), may hold values from 0 to 1, as said below
- spectra: float32 [36, 32, 128, 256], P(None, None, ('groups', 'tile'), 'col'), may hold values from 0.1 to 3
- wind_speed: float32 [128, 256], P(('groups', 'tile'), 'col'), may hold values from 1 to 10
- wind_direction: float32 [128, 256], P(('groups', 'tile'), 'col'), may hold values from -3.140625 to 3.140625
- wave_wet: int32 [128, 256], P(('groups', 'tile'), 'col'), may hold values from 0 to 1, as said below
- remap_source: int32 [32, 8, 512], P(('groups', 'tile', 'col')), may hold values from 0 to 4096, as said below
- remap_target: int32 [32, 8, 512], P(('groups', 'tile', 'col')), may hold values from 0 to 1024, as said below
- remap_weight: float32 [32, 8, 512], P(('groups', 'tile', 'col')), as said below
Outputs:
- new_zonal: float32 [50, 512, 256], P(None, ('groups', 'tile'), 'col')
- new_meridional: float32 [50, 512, 256], P(None, ('groups', 'tile'), 'col')
- new_height: float32 [512, 256], P(('groups', 'tile'), 'col')
- new_spectra: float32 [36, 32, 128, 256], P(None, None, ('groups', 'tile'), 'col')
The draws below stay inside these ranges and needn't reach their ends.
Inputs may be any that keep to these rules, and one draw needn't show every extreme that they name: `ocean_wet`: 1 marks sea. `wave_wet`: 1 exactly where the 2x2 block of ocean cells under the wave cell (ocean rows 2y, 2y+1, columns 2x, 2x+1) holds sea. `remap_source`: block [s, j] lists, in row-major order and from slot 0 on, the sea cells of rank s in its local columns j * 2 * 8 to (j + 1) * 2 * 8 - 1, as local index row * 128 + column; the remaining slots hold 4096. Every sea cell appears in exactly one entry. In every draw some rank holds the wave cells of 8 full blocks, one from each rank that sends to it. `remap_target`: for each live entry the wave cell on rank d that the entry links to, as local index column * 128 + row, in the slot of the entry in its source block; padded entries hold 1024. `remap_weight`: positive on live entries, summing to 1 over the entries that end in one wave cell; 0 on padded entries.
All inputs are finite; a program needn't handle non-finite values.
Results may differ from the reference program's by a relative error of at most 0.00015.
Values sent between devices are 32-bit elements; how exact they have to be, the bound alone decides.
A program may use at most 192 MiB of HBM per device.

```python
import math
import jax
import jax.numpy as jnp
from jax import lax

LEV = 50
ND = 36
NF = 32
OR = 32
OC = 128
WSTEPS = 4
OSTEPS = 4
SPLIT = 2
RANKS = 32
NYO = 512
NXO = 256
XW = 8
YW = 128
NXW = 128
NYW = 256
PEERS = 8
SLOTS = 512


def coast_mask(key):
    key = jax.random.fold_in(key, 101)
    block_key, cell_key, pick_key = jax.random.split(key, 3)
    tile_count = NYO // OR
    col_count = NXO // OC
    block_wet = jax.random.randint(block_key, (NYO // 2, NXO // 2), 0, 8) != 0
    chosen = jax.random.randint(pick_key, (), 0, tile_count * col_count)
    wave_rows = jnp.arange(NYO // 2, dtype=jnp.int32)[:, None]
    wave_cols = jnp.arange(NXO // 2, dtype=jnp.int32)[None, :]
    full_block = (wave_rows // YW == chosen % col_count) & (wave_cols // XW == chosen // col_count)
    block_wet = block_wet | full_block
    cell_draw = jax.random.randint(cell_key, (NYO, NXO), 0, 8) != 0
    corner_cell = (jnp.arange(NYO)[:, None] % 2 == 0) & (jnp.arange(NXO)[None, :] % 2 == 0)
    spread_wet = jnp.repeat(jnp.repeat(block_wet, 2, axis=0), 2, axis=1)
    spread_full = jnp.repeat(jnp.repeat(full_block, 2, axis=0), 2, axis=1)
    ocean = spread_wet & (cell_draw | corner_cell | spread_full)
    return (ocean.astype(jnp.int32), block_wet.astype(jnp.int32))


def by_group(values):
    tile_count = NYO // OR
    col_count = NXO // OC
    shaped = values.reshape(tile_count, OR, col_count, PEERS, SLOTS // OR)
    return jnp.transpose(shaped, (0, 2, 3, 1, 4)).reshape(tile_count * col_count, PEERS, SLOTS)


def remap_lists(key):
    ocean, blocks = coast_mask(key)
    area_key = jax.random.fold_in(key, 102)
    shift_key = jax.random.fold_in(key, 103)
    col_count = NXO // OC
    area_factor = jax.random.uniform(area_key, (NYO, NXO), jnp.float32, 0.5, 1.5)
    shifts = jax.random.randint(shift_key, (2, NYO, NXO), -1, 2)
    row_grid = jnp.arange(NYO, dtype=jnp.int32)[:, None] + jnp.zeros((1, NXO), jnp.int32)
    col_grid = jnp.arange(NXO, dtype=jnp.int32)[None, :] + jnp.zeros((NYO, 1), jnp.int32)
    strip_rows = OR // 2
    lowest_row = row_grid // OR * strip_rows
    target_row = jnp.clip(row_grid // 2 + shifts[0], lowest_row, lowest_row + strip_rows - 1)
    lowest_col = col_grid // (2 * XW) * XW
    target_col = jnp.clip(col_grid // 2 + shifts[1], lowest_col, lowest_col + XW - 1)
    wave_index = target_col * NYW + target_row
    live_cells = ocean > 0
    wet_area = area_factor * ocean.astype(jnp.float32)
    totals = jax.ops.segment_sum(wet_area.reshape(NYO * NXO), wave_index.reshape(NYO * NXO), num_segments=NXW * NYW)
    cell_total = totals[wave_index]
    cell_share = jnp.where(live_cells, wet_area / jnp.where(cell_total > 0, cell_total, 1.0), 0.0)
    local_cell = row_grid % OR * OC + col_grid % OC
    local_target = target_col % XW * YW + target_row % YW
    live_slot = by_group(ocean)
    slot_index = jnp.where(live_slot > 0, jnp.cumsum(live_slot, axis=-1) - 1, SLOTS)
    rank_ids = jnp.arange(RANKS, dtype=jnp.int32)[:, None, None]
    peer_ids = jnp.arange(PEERS, dtype=jnp.int32)[None, :, None]

    def packed(values, filler):
        holder = jnp.full((RANKS, PEERS, SLOTS + 1), filler, values.dtype)
        return holder.at[rank_ids, peer_ids, slot_index].set(by_group(values))[:, :, :SLOTS]
    source_rows = packed(local_cell, OR * OC)
    target_rows = packed(local_target, XW * YW)
    weight_rows = packed(cell_share, 0.0)
    target_by_dest = target_rows.reshape(col_count, PEERS, col_count, PEERS, SLOTS).transpose(2, 3, 0, 1, 4).reshape(RANKS, PEERS, SLOTS)
    return (source_rows, target_by_dest, weight_rows)


def draw_ocean_wet(key, part):
    return coast_mask(key)[0]


def draw_wave_wet(key, part):
    return jnp.transpose(coast_mask(key)[1])


def draw_remap_source(key, part):
    return remap_lists(key)[0]


def draw_remap_target(key, part):
    return remap_lists(key)[1]


def draw_remap_weight(key, part):
    return remap_lists(key)[2]


def block_scale(key, dims, cuts, smallest, high):
    loudness, own = 1.0, jax.random.fold_in(key, 6)
    for axis_at, parts in cuts:
        steps = jnp.exp(jax.random.uniform(jax.random.fold_in(own, axis_at), (parts,), jnp.float32, smallest / len(cuts), high / len(cuts)))
        loudness = loudness * jnp.repeat(steps, dims[axis_at] // parts).reshape([-1 if axis == axis_at else 1 for axis in range(len(dims))])
    return loudness


def scatter_about(stream_key, shape, width, bound, pieces=(), kind=jnp.bfloat16):
    entries = jax.random.normal(stream_key, shape, jnp.float32) * width
    if len(pieces) > 0:
        entries = block_scale(stream_key, shape, pieces, -0.22, 0.18) * entries
    return jnp.clip(entries, min=-bound, max=bound).astype(kind)


def setup_inputs(seed: int = 0, part: int = 0) -> dict:
    keys = jax.random.split(jax.random.key(seed), 14)
    own_keys = jax.random.split(jax.random.fold_in(keys[13], part), 14)
    zonal_velocity = scatter_about(own_keys[0], (LEV, NYO, NXO), 1.0, 4.0, ((1, 16), (2, 2)), jnp.float32)
    meridional_velocity = scatter_about(own_keys[1], (LEV, NYO, NXO), 1.0, 4.0, ((1, 16), (2, 2)), jnp.float32)
    surface_height = scatter_about(own_keys[2], (NYO, NXO), 1.0, 3.0, ((0, 16), (1, 2)), jnp.float32)
    thickness = jnp.clip(jnp.exp(jax.random.uniform(keys[3], (LEV,), jnp.float32, math.log(0.5), math.log(2.0))), 0.5, 2.0)
    mixing = jnp.clip(jnp.exp(jax.random.uniform(keys[4], (LEV,), jnp.float32, math.log(0.02), math.log(0.2))), 0.02, 0.2)
    ocean_wet = draw_ocean_wet(jax.random.fold_in(jax.random.fold_in(keys[13], part), 71), part)
    spectra = jnp.clip(jnp.exp(math.log(3.0) - 3.4011974 * jax.random.uniform(own_keys[6], (ND, NF, NXW, NYW), jnp.float32) ** block_scale(own_keys[6], (ND, NF, NXW, NYW), ((2, 16), (3, 2)), -0.2, 0.2)), 0.1, 3.0)
    wind_speed = jnp.clip(jnp.exp(math.log(10.0) - 2.3025851 * jax.random.uniform(own_keys[7], (NXW, NYW), jnp.float32) ** block_scale(own_keys[7], (NXW, NYW), ((0, 16), (1, 2)), -0.2, 0.2)), 1.0, 10.0)
    wind_direction = jnp.clip(jax.random.uniform(own_keys[8], (NXW, NYW), jnp.float32, -3.140625, 3.140625), -3.140625, 3.140625)
    wave_wet = draw_wave_wet(jax.random.fold_in(jax.random.fold_in(keys[13], part), 71), part)
    remap_source = draw_remap_source(jax.random.fold_in(jax.random.fold_in(keys[13], part), 71), part)
    remap_target = draw_remap_target(jax.random.fold_in(jax.random.fold_in(keys[13], part), 71), part)
    remap_weight = draw_remap_weight(jax.random.fold_in(jax.random.fold_in(keys[13], part), 71), part)
    return {"zonal_velocity": zonal_velocity, "meridional_velocity": meridional_velocity, "surface_height": surface_height, "thickness": thickness, "mixing": mixing, "ocean_wet": ocean_wet, "spectra": spectra, "wind_speed": wind_speed, "wind_direction": wind_direction, "wave_wet": wave_wet, "remap_source": remap_source, "remap_target": remap_target, "remap_weight": remap_weight}


def spectral_tables():
    angles = (jnp.arange(ND, dtype=jnp.float32) + 0.5) * (2.0 * math.pi / ND)
    group_speed = 0.5 * jnp.power(jnp.float32(1.1), -jnp.arange(NF, dtype=jnp.float32))
    freq_weight = 2.0 * (jnp.arange(NF, dtype=jnp.float32) + 1.0) / NF
    return jnp.cos(angles), jnp.sin(angles), group_speed, freq_weight


def source_term(energy, fields, tables):
    cos_dir, sin_dir, group_speed, freq_weight = tables
    downwind = jnp.maximum(fields[3][None] * cos_dir[:, None, None] + fields[4][None] * sin_dir[:, None, None], 0.0)
    column_mean = jnp.mean(energy, axis=(0, 1))
    damping = 0.3 * jnp.exp(-0.5 * fields[5]) * column_mean
    growth = 0.02 * downwind[:, None] * freq_weight[None, :, None, None] - damping[None, None]
    return energy * jnp.exp(growth)


def advect(padded, fields, tables):
    cos_dir, sin_dir, group_speed, freq_weight = tables
    drift_x, drift_y, wet_cells = fields[0], fields[1], fields[2]
    speed_grid = group_speed[None, :, None, None]
    velocity_x = speed_grid * cos_dir[:, None, None, None] + drift_x[None, None]
    velocity_y = speed_grid * sin_dir[:, None, None, None] + drift_y[None, None]
    face_x = 0.5 * (velocity_x[:, :, :-1, 1:-1] + velocity_x[:, :, 1:, 1:-1])
    open_x = wet_cells[:-1, 1:-1] * wet_cells[1:, 1:-1]
    flux_x = (jnp.maximum(face_x, 0.0) * padded[:, :, :-1, 1:-1] + jnp.minimum(face_x, 0.0) * padded[:, :, 1:, 1:-1]) * open_x
    face_y = 0.5 * (velocity_y[:, :, 1:-1, :-1] + velocity_y[:, :, 1:-1, 1:])
    open_y = wet_cells[1:-1, :-1] * wet_cells[1:-1, 1:]
    flux_y = (jnp.maximum(face_y, 0.0) * padded[:, :, 1:-1, :-1] + jnp.minimum(face_y, 0.0) * padded[:, :, 1:-1, 1:]) * open_y
    return padded[:, :, 1:-1, 1:-1] - (flux_x[:, :, 1:] - flux_x[:, :, :-1]) - (flux_y[:, :, :, 1:] - flux_y[:, :, :, :-1])


def radiation_stress(energy, tables):
    cos_dir, sin_dir = tables[0], tables[1]
    moments = jnp.stack([cos_dir * cos_dir, cos_dir * sin_dir, sin_dir * sin_dir]) * (0.5 / (ND * NF))
    per_direction = jnp.sum(energy, axis=1)
    return jnp.einsum("cd,dxy->cxy", moments, per_direction, precision=lax.Precision.HIGHEST)


def mixing_tendency(profile, top_force, mixing, thickness):
    interface_flux = mixing[1:, None, None] * (profile[:-1] - profile[1:])
    bottom = mixing[0] * profile[-1:]
    fluxes = jnp.concatenate([top_force[None], interface_flux, bottom], axis=0)
    return (fluxes[:-1] - fluxes[1:]) / thickness[:, None, None]


def centered(extended):
    slope_x = 0.5 * (extended[..., 1:-1, 2:] - extended[..., 1:-1, :-2])
    slope_y = 0.5 * (extended[..., 2:, 1:-1] - extended[..., :-2, 1:-1])
    return slope_x, slope_y


def padded_plane(values):
    return jnp.pad(values, [(0, 0)] * (values.ndim - 2) + [(1, 1), (1, 1)])


def global_links(remap_source, remap_target):
    by_source = remap_target.reshape(SPLIT, PEERS, SPLIT, PEERS, SLOTS).transpose(2, 3, 0, 1, 4).reshape(RANKS, PEERS, SLOTS)
    rank_ids = jnp.arange(RANKS, dtype=jnp.int32)
    peer_ids = jnp.arange(PEERS, dtype=jnp.int32)[None, :, None]
    from_tile = (rank_ids // SPLIT)[:, None, None]
    from_col = (rank_ids % SPLIT)[:, None, None]
    dest_tile = from_col * PEERS + peer_ids
    dest_col = from_tile // PEERS
    source_clip = jnp.minimum(remap_source, OR * OC - 1)
    ocean_cell = (from_tile * OR + source_clip // OC) * NXO + from_col * OC + source_clip % OC
    ocean_cell = jnp.where(remap_source == OR * OC, NYO * NXO, ocean_cell).astype(jnp.int32)
    target_clip = jnp.minimum(by_source, XW * YW - 1)
    wave_cell = (dest_tile * XW + target_clip // YW) * NYW + dest_col * YW + target_clip % YW
    wave_cell = jnp.where(by_source == XW * YW, NXW * NYW, wave_cell).astype(jnp.int32)
    return ocean_cell, wave_cell


def reference(zonal_velocity, meridional_velocity, surface_height, thickness, mixing, ocean_wet, spectra, wind_speed, wind_direction, wave_wet, remap_source, remap_target, remap_weight):
    tables = spectral_tables()
    sea_cells = ocean_wet.astype(jnp.float32)
    wet_cells = wave_wet.astype(jnp.float32)
    zonal_flow = zonal_velocity * sea_cells[None]
    meridional = meridional_velocity * sea_cells[None]
    ocean_cell, wave_cell = global_links(remap_source, remap_target)
    surface = jnp.stack([zonal_flow[0], meridional[0], surface_height]).reshape(3, NYO * NXO)
    surface = jnp.concatenate([surface, jnp.zeros((3, 1), jnp.float32)], axis=1)
    linked = surface[:, ocean_cell] * remap_weight[None]
    currents = jnp.zeros((3, NXW * NYW + 1), jnp.float32).at[:, wave_cell].add(linked)
    currents = currents[:, :-1].reshape(3, NXW, NYW)
    energy = spectra * wet_cells[None, None]
    stress = radiation_stress(energy, tables).reshape(3, NXW * NYW)
    stress = jnp.concatenate([stress, jnp.zeros((3, 1), jnp.float32)], axis=1)
    ocean_stress = jnp.zeros((3, NYO * NXO + 1), jnp.float32).at[:, ocean_cell].add(stress[:, wave_cell])
    ocean_stress = ocean_stress[:, :-1].reshape(3, NYO, NXO)
    fields = jnp.stack([0.03 * currents[0], 0.03 * currents[1], wet_cells, wind_speed * jnp.cos(wind_direction), wind_speed * jnp.sin(wind_direction), currents[2]])
    edged_fields = padded_plane(fields)
    for section_index in range(WSTEPS):
        energy = source_term(energy, fields, tables)
        energy = advect(padded_plane(energy), edged_fields, tables)
    slope_x, slope_y = centered(padded_plane(ocean_stress))
    force_x = -0.5 * (slope_x[0] + slope_y[1])
    force_y = -0.5 * (slope_x[1] + slope_y[2])
    coriolis = (0.1 + 0.1 * (jnp.arange(NYO).astype(jnp.float32) + 0.5) / NYO)[:, None]
    column_depth = jnp.sum(thickness)
    height = surface_height
    for iteration in range(OSTEPS):
        transport_x = jnp.sum(thickness[:, None, None] * zonal_flow, axis=0) / column_depth
        transport_y = jnp.sum(thickness[:, None, None] * meridional, axis=0) / column_depth
        diverge_x = centered(padded_plane(transport_x))[0]
        diverge_y = centered(padded_plane(transport_y))[1]
        new_height = height - 0.2 * (diverge_x + diverge_y)
        slope_x, slope_y = centered(padded_plane(new_height))
        pressure_x = 0.2 * slope_x
        pressure_y = 0.2 * slope_y
        new_zonal = (zonal_flow + coriolis * meridional - pressure_x + mixing_tendency(zonal_flow, force_x, mixing, thickness)) * sea_cells[None]
        new_meridional = (meridional - coriolis * zonal_flow - pressure_y + mixing_tendency(meridional, force_y, mixing, thickness)) * sea_cells[None]
        zonal_flow, meridional, height = new_zonal, new_meridional, new_height
    return zonal_flow, meridional, height, energy
```

```python
import math

import jax
import jax.numpy as jnp
from jax import lax
from jax.experimental import pallas as pl
from jax.experimental.pallas import tpu as pltpu
from jax.sharding import PartitionSpec as P

ND = 36
NF = 32
WSTEPS = 4
OSTEPS = 4


def padded_2(value, sides, width):
    for axis, dim in sides:
        count, length = (lax.axis_size(axis), value.shape[dim])
        up = [(i, (i + 1) % count) for i in range(count - 1)]
        down = [(j, i) for i, j in up]
        last = lax.slice_in_dim(value, length - width, length, axis=dim)
        initial = lax.slice_in_dim(value, 0, width, axis=dim)
        before = lax.ppermute(last, axis, up)
        after = lax.ppermute(initial, axis, down)
        value = jnp.concatenate([before, value, after], axis=dim)
    return value


def spectral_tables():
    angles = (jnp.arange(ND, dtype=jnp.float32) + 0.5) * (2.0 * math.pi / ND)
    group_speed = 0.5 * jnp.power(jnp.float32(1.1), -jnp.arange(NF, dtype=jnp.float32))
    freq_weight = 2.0 * (jnp.arange(NF, dtype=jnp.float32) + 1.0) / NF
    return (jnp.cos(angles), jnp.sin(angles), group_speed, freq_weight)


def source_term(energy, fields, tables):
    cos_dir, sin_dir, group_speed, freq_weight = tables
    downwind = jnp.maximum(
        fields[3][None] * cos_dir[:, None, None] + fields[4][None] * sin_dir[:, None, None], 0.0
    )
    column_mean = jnp.mean(energy, axis=(0, 1))
    damping = 0.3 * jnp.exp(-0.5 * fields[5]) * column_mean
    growth = 0.02 * downwind[:, None] * freq_weight[None, :, None, None] - damping[None, None]
    return energy * jnp.exp(growth)


def advect(padded, fields, tables):
    cos_dir, sin_dir, group_speed, freq_weight = tables
    drift_x, drift_y, wet_cells = (fields[0], fields[1], fields[2])
    speed_grid = group_speed[None, :, None, None]
    velocity_x = speed_grid * cos_dir[:, None, None, None] + drift_x[None, None]
    velocity_y = speed_grid * sin_dir[:, None, None, None] + drift_y[None, None]
    face_x = 0.5 * (velocity_x[:, :, :-1, 1:-1] + velocity_x[:, :, 1:, 1:-1])
    open_x = wet_cells[:-1, 1:-1] * wet_cells[1:, 1:-1]
    flux_x = (
        jnp.maximum(face_x, 0.0) * padded[:, :, :-1, 1:-1]
        + jnp.minimum(face_x, 0.0) * padded[:, :, 1:, 1:-1]
    ) * open_x
    face_y = 0.5 * (velocity_y[:, :, 1:-1, :-1] + velocity_y[:, :, 1:-1, 1:])
    open_y = wet_cells[1:-1, :-1] * wet_cells[1:-1, 1:]
    flux_y = (
        jnp.maximum(face_y, 0.0) * padded[:, :, 1:-1, :-1]
        + jnp.minimum(face_y, 0.0) * padded[:, :, 1:-1, 1:]
    ) * open_y
    return (
        padded[:, :, 1:-1, 1:-1]
        - (flux_x[:, :, 1:] - flux_x[:, :, :-1])
        - (flux_y[:, :, :, 1:] - flux_y[:, :, :, :-1])
    )


def radiation_stress(energy, tables):
    cos_dir, sin_dir = (tables[0], tables[1])
    moments = jnp.stack([cos_dir * cos_dir, cos_dir * sin_dir, sin_dir * sin_dir]) * (
        0.5 / (ND * NF)
    )
    per_direction = jnp.sum(energy, axis=1)
    return jnp.einsum("cd,dxy->cxy", moments, per_direction, precision=lax.Precision.HIGHEST)


def mixing_tendency(profile, top_force, mixing, thickness):
    interface_flux = mixing[1:, None, None] * (profile[:-1] - profile[1:])
    bottom = mixing[0] * profile[-1:]
    fluxes = jnp.concatenate([top_force[None], interface_flux, bottom], axis=0)
    return (fluxes[:-1] - fluxes[1:]) / thickness[:, None, None]


def centered(extended):
    slope_x = 0.5 * (extended[..., 1:-1, 2:] - extended[..., 1:-1, :-2])
    slope_y = 0.5 * (extended[..., 2:, 1:-1] - extended[..., :-2, 1:-1])
    return (slope_x, slope_y)


def split_parts(x):
    high = x.astype(jnp.bfloat16).astype(jnp.float32)
    rest = x - high
    middle = rest.astype(jnp.bfloat16).astype(jnp.float32)
    low = rest - middle
    return jnp.concatenate([high, middle, low], axis=0).astype(jnp.bfloat16)


def join_parts(r):
    return r[0:8] + r[8:16] + r[16:24]


def block_onehot(source_row, j, row_length, width):
    cells = source_row.shape[1]
    n = lax.broadcasted_iota(jnp.int32, (cells, cells), 0)
    ids = (n // width) * row_length + j * width + n % width
    return jnp.where(ids == source_row, 1.0, 0.0).astype(jnp.bfloat16)


def wave_onehot(target_row, cells):
    n = lax.broadcasted_iota(jnp.int32, (cells, target_row.shape[1]), 0)
    return jnp.where(n == target_row, 1.0, 0.0).astype(jnp.bfloat16)


NN = (((1,), (0,)), ((), ()))
NT = (((1,), (1,)), ((), ()))


def gather_kernel(row_length, width, spectra, wet, surface, source, target, weight, out, flat):
    span_x, span_y = wet.shape
    peers = source.shape[0]
    zero = jnp.zeros((span_x, span_y), jnp.float32)
    acc = [zero, zero, zero]
    for d in range(ND):
        theta = (d + 0.5) * (2.0 * math.pi / ND)
        part = jnp.sum(spectra[d], axis=0)
        cos, sin = math.cos(theta), math.sin(theta)
        for c, m in enumerate((cos * cos, cos * sin, sin * sin)):
            acc[c] = acc[c] + part * (m * 0.5 / (ND * NF))
    wetf = wet[...].astype(jnp.float32)
    flat[...] = jnp.zeros_like(flat)
    for c in range(3):
        plane = acc[c] * wetf
        for x in range(span_x):
            flat[3 + c : 4 + c, x * span_y : (x + 1) * span_y] = plane[x : x + 1, :]
    stress = split_parts(flat[...])

    def step(j, carry):
        hot = block_onehot(source[j], j, row_length, width)
        values = join_parts(
            lax.dot_general(split_parts(surface[j]), hot, NN, preferred_element_type=jnp.float32)
        )
        hot2 = wave_onehot(target[j], span_x * span_y)
        back = join_parts(
            lax.dot_general(stress, hot2, NN, preferred_element_type=jnp.float32)
        )
        out[j] = values * weight[j] + back
        return carry

    lax.fori_loop(0, peers, step, 0)


def swap_kernel(src, dst, send_sem, recv_sem, local_sem):
    peers = src.shape[0]
    t = lax.axis_index("tile")
    c = lax.axis_index("col")
    side = t // peers
    slot = lax.rem(t, peers)
    barrier = pltpu.get_barrier_semaphore()

    def partner(j):
        return {"tile": c * peers + j, "col": side}

    def copy(j):
        return pltpu.make_async_remote_copy(
            src_ref=src.at[j],
            dst_ref=dst.at[slot],
            send_sem=send_sem.at[j],
            recv_sem=recv_sem.at[slot],
            device_id=partner(j),
            device_id_type=pl.DeviceIdType.MESH,
        )

    def arrival(j):
        return pltpu.make_async_remote_copy(
            src_ref=src.at[j],
            dst_ref=dst.at[j],
            send_sem=send_sem.at[j],
            recv_sem=recv_sem.at[j],
            device_id=partner(j),
            device_id_type=pl.DeviceIdType.MESH,
        )

    def other(j):
        return jnp.logical_or(side != c, slot != j)

    for j in range(peers):

        @pl.when(other(j))
        def _():
            pl.semaphore_signal(
                barrier, inc=1, device_id=partner(j), device_id_type=pl.DeviceIdType.MESH
            )

    @pl.when(side == c)
    def _():
        pl.semaphore_wait(barrier, peers - 1)

    @pl.when(side != c)
    def _():
        pl.semaphore_wait(barrier, peers)

    for j in range(peers):

        @pl.when(other(j))
        def _():
            copy(j).start()

        @pl.when(jnp.logical_not(other(j)))
        def _():
            own = pltpu.make_async_copy(src.at[j], dst.at[j], local_sem)
            own.start()
            own.wait()

    for j in range(peers):

        @pl.when(other(j))
        def _():
            copy(j).wait_send()
            arrival(j).wait_recv()


def scatter_kernel(row_length, width, arrived, source, target, waves, ocean):
    peers = source.shape[0]
    waves[...] = jnp.zeros_like(waves)

    def step(j, carry):
        parts = split_parts(arrived[j])
        hot = block_onehot(source[j], j, row_length, width)
        ocean[j] = join_parts(
            lax.dot_general(parts, hot, NT, preferred_element_type=jnp.float32)
        )
        hot2 = wave_onehot(target[j], waves.shape[1])
        waves[...] += join_parts(
            lax.dot_general(parts, hot2, NT, preferred_element_type=jnp.float32)
        )
        return carry

    lax.fori_loop(0, peers, step, 0)


VMEM = pl.BlockSpec(memory_space=pltpu.VMEM)


def remap(spectra, wave_wet, surface, remap_source, remap_target, remap_weight):
    peers, slots = remap_source.shape[1:]
    span_x, span_y = wave_wet.shape
    rows, cols = surface.shape[1:]
    width = cols // peers
    source = remap_source.reshape(peers, 1, slots)
    target = remap_target.reshape(peers, 1, slots)
    weight = remap_weight.reshape(peers, 1, slots)
    blocks = surface.reshape(3, rows, peers, width).transpose(2, 0, 1, 3).reshape(peers, 3, slots)
    blocks = jnp.concatenate([blocks, jnp.zeros((peers, 5, slots), jnp.float32)], axis=1)
    shape = jax.ShapeDtypeStruct((peers, 8, slots), jnp.float32)
    sent = pl.pallas_call(
        lambda *refs: gather_kernel(cols, width, *refs),
        out_shape=shape,
        in_specs=[VMEM] * 6,
        out_specs=VMEM,
        scratch_shapes=[pltpu.VMEM((8, span_x * span_y), jnp.float32)],
        compiler_params=pltpu.CompilerParams(vmem_limit_bytes=32 * 1024 * 1024),
    )(spectra, wave_wet, blocks, source, target, weight)
    arrived = pl.pallas_call(
        swap_kernel,
        out_shape=shape,
        in_specs=[VMEM],
        out_specs=VMEM,
        scratch_shapes=[
            pltpu.SemaphoreType.DMA((peers,)),
            pltpu.SemaphoreType.DMA((peers,)),
            pltpu.SemaphoreType.DMA,
        ],
        compiler_params=pltpu.CompilerParams(collective_id=0, has_side_effects=True),
    )(sent)
    waves, ocean = pl.pallas_call(
        lambda *refs: scatter_kernel(cols, width, *refs),
        out_shape=(jax.ShapeDtypeStruct((8, span_x * span_y), jnp.float32), shape),
        in_specs=[VMEM] * 3,
        out_specs=(VMEM, VMEM),
        compiler_params=pltpu.CompilerParams(vmem_limit_bytes=32 * 1024 * 1024),
    )(arrived, source, target)
    currents = waves[:3].reshape(3, span_x, span_y)
    ocean_stress = (
        ocean[:, 3:6]
        .reshape(peers, 3, rows, width)
        .transpose(1, 2, 0, 3)
        .reshape(3, rows, cols)
    )
    return currents, ocean_stress


def body(
    zonal_velocity,
    meridional_velocity,
    surface_height,
    thickness,
    mixing,
    ocean_wet,
    spectra,
    wind_speed,
    wind_direction,
    wave_wet,
    remap_source,
    remap_target,
    remap_weight,
):
    tables = spectral_tables()
    tile_count = lax.axis_size("tile")
    col_count = lax.axis_size("col")
    tile_rows, tile_cols = surface_height.shape
    sea_cells = ocean_wet.astype(jnp.float32)
    wet_cells = wave_wet.astype(jnp.float32)
    zonal_flow = zonal_velocity * sea_cells[None]
    meridional = meridional_velocity * sea_cells[None]
    height = surface_height
    energy = spectra * wet_cells[None, None]
    surface = jnp.stack([zonal_flow[0], meridional[0], height])
    currents, ocean_stress = remap(
        spectra, wave_wet, surface, remap_source, remap_target, remap_weight
    )
    fields = jnp.stack(
        [
            0.03 * currents[0],
            0.03 * currents[1],
            wet_cells,
            wind_speed * jnp.cos(wind_direction),
            wind_speed * jnp.sin(wind_direction),
            currents[2],
        ]
    )
    wide_fields = padded_2(fields, (("tile", 1), ("col", 2)), 2)
    inner_fields = wide_fields[:, 1:-1, 1:-1]
    for section_index in range(WSTEPS):
        energy = source_term(energy, fields, tables)
        padded = padded_2(energy, (("tile", 2), ("col", 3)), 1)
        energy = advect(padded, inner_fields, tables)
    row_start = lax.axis_index("tile") * tile_rows
    col_start = lax.axis_index("col") * tile_cols
    total_rows = tile_rows * tile_count
    total_cols = tile_cols * col_count
    coriolis = (
        0.1 + 0.1 * ((row_start + jnp.arange(tile_rows)).astype(jnp.float32) + 0.5) / total_rows
    )[:, None]
    edge_rows = row_start + jnp.arange(-1, tile_rows + 1)
    edge_cols = col_start + jnp.arange(-1, tile_cols + 1)
    inside = (
        ((edge_rows >= 0) & (edge_rows < total_rows))[:, None]
        & ((edge_cols >= 0) & (edge_cols < total_cols))[None, :]
    ).astype(jnp.float32)
    column_depth = jnp.sum(thickness)
    force_x = jnp.zeros_like(height)
    force_y = jnp.zeros_like(height)
    for iteration in range(OSTEPS):
        transport_x = jnp.sum(thickness[:, None, None] * zonal_flow, axis=0) / column_depth
        transport_y = jnp.sum(thickness[:, None, None] * meridional, axis=0) / column_depth
        carried = jnp.stack([transport_x, transport_y, height])
        if iteration == 0:
            carried = jnp.concatenate([carried, ocean_stress], axis=0)
        border = padded_2(carried, (("tile", 1), ("col", 2)), 2)
        if iteration == 0:
            slope_x, slope_y = centered(border[3:, 1:-1, 1:-1])
            force_x = -0.5 * (slope_x[0] + slope_y[1])
            force_y = -0.5 * (slope_x[1] + slope_y[2])
        diverge_x = 0.5 * (border[0, 1:-1, 2:] - border[0, 1:-1, :-2])
        diverge_y = 0.5 * (border[1, 2:, 1:-1] - border[1, :-2, 1:-1])
        margin_height = (border[2, 1:-1, 1:-1] - 0.2 * (diverge_x + diverge_y)) * inside
        slope_x, slope_y = centered(margin_height)
        pressure_x = 0.2 * slope_x
        pressure_y = 0.2 * slope_y
        new_zonal = (
            zonal_flow
            + coriolis * meridional
            - pressure_x
            + mixing_tendency(zonal_flow, force_x, mixing, thickness)
        ) * sea_cells[None]
        new_meridional = (
            meridional
            - coriolis * zonal_flow
            - pressure_y
            + mixing_tendency(meridional, force_y, mixing, thickness)
        ) * sea_cells[None]
        zonal_flow, meridional = (new_zonal, new_meridional)
        height = margin_height[1:-1, 1:-1]
    return (zonal_flow, meridional, height, energy)


def solution(mesh):
    return jax.shard_map(
        body,
        mesh=mesh,
        in_specs=(
            P(None, ("groups", "tile"), "col"),
            P(None, ("groups", "tile"), "col"),
            P(("groups", "tile"), "col"),
            P(),
            P(),
            P(("groups", "tile"), "col"),
            P(None, None, ("groups", "tile"), "col"),
            P(("groups", "tile"), "col"),
            P(("groups", "tile"), "col"),
            P(("groups", "tile"), "col"),
            P(("groups", "tile", "col"), None, None),
            P(("groups", "tile", "col"), None, None),
            P(("groups", "tile", "col"), None, None),
        ),
        out_specs=(
            P(None, ("groups", "tile"), "col"),
            P(None, ("groups", "tile"), "col"),
            P(("groups", "tile"), "col"),
            P(None, None, ("groups", "tile"), "col"),
        ),
        check_vma=False,
    )
```

```python
import math

import jax
import jax.numpy as jnp
from jax import lax
from jax.experimental import pallas as pl
from jax.experimental.pallas import tpu as pltpu
from jax.sharding import PartitionSpec as P

ND = 36
NF = 32
WSTEPS = 4
OSTEPS = 4


def spectral_tables():
    angles = (jnp.arange(ND, dtype=jnp.float32) + 0.5) * (2.0 * math.pi / ND)
    group_speed = 0.5 * jnp.power(jnp.float32(1.1), -jnp.arange(NF, dtype=jnp.float32))
    freq_weight = 2.0 * (jnp.arange(NF, dtype=jnp.float32) + 1.0) / NF
    return (jnp.cos(angles), jnp.sin(angles), group_speed, freq_weight)


def split_parts(x):
    high = x.astype(jnp.bfloat16).astype(jnp.float32)
    rest = x - high
    middle = rest.astype(jnp.bfloat16).astype(jnp.float32)
    low = rest - middle
    return jnp.concatenate([high, middle, low], axis=0).astype(jnp.bfloat16)


def join_parts(r):
    return r[0:8] + r[8:16] + r[16:24]


def block_onehot(source_row, j, row_length, width):
    cells = source_row.shape[1]
    n = lax.broadcasted_iota(jnp.int32, (cells, cells), 0)
    ids = (n // width) * row_length + j * width + n % width
    return jnp.where(ids == source_row, 1.0, 0.0).astype(jnp.bfloat16)


def wave_onehot(target_row, cells):
    n = lax.broadcasted_iota(jnp.int32, (cells, target_row.shape[1]), 0)
    return jnp.where(n == target_row, 1.0, 0.0).astype(jnp.bfloat16)


NN = (((1,), (0,)), ((), ()))
NT = (((1,), (1,)), ((), ()))


def gather_kernel(row_length, width, spectra, wet, surface, source, target, weight, out, flat):
    span_x, span_y = wet.shape
    peers = source.shape[0]
    zero = jnp.zeros((span_x, span_y), jnp.float32)
    acc = [zero, zero, zero]
    for d in range(ND):
        theta = (d + 0.5) * (2.0 * math.pi / ND)
        part = jnp.sum(spectra[d], axis=0)
        cos, sin = math.cos(theta), math.sin(theta)
        for c, m in enumerate((cos * cos, cos * sin, sin * sin)):
            acc[c] = acc[c] + part * (m * 0.5 / (ND * NF))
    wetf = wet[...].astype(jnp.float32)
    flat[...] = jnp.zeros_like(flat)
    for c in range(3):
        plane = acc[c] * wetf
        for x in range(span_x):
            flat[3 + c : 4 + c, x * span_y : (x + 1) * span_y] = plane[x : x + 1, :]
    stress = split_parts(flat[...])

    def step(j, carry):
        hot = block_onehot(source[j], j, row_length, width)
        values = join_parts(
            lax.dot_general(split_parts(surface[j]), hot, NN, preferred_element_type=jnp.float32)
        )
        hot2 = wave_onehot(target[j], span_x * span_y)
        back = join_parts(
            lax.dot_general(stress, hot2, NN, preferred_element_type=jnp.float32)
        )
        out[j] = values * weight[j] + back
        return carry

    lax.fori_loop(0, peers, step, 0)


def swap_kernel(src, dst, send_sem, recv_sem, local_sem):
    peers = src.shape[0]
    t = lax.axis_index("tile")
    c = lax.axis_index("col")
    side = t // peers
    slot = lax.rem(t, peers)
    barrier = pltpu.get_barrier_semaphore()

    def partner(j):
        return {"tile": c * peers + j, "col": side}

    def copy(j):
        return pltpu.make_async_remote_copy(
            src_ref=src.at[j],
            dst_ref=dst.at[slot],
            send_sem=send_sem.at[j],
            recv_sem=recv_sem.at[slot],
            device_id=partner(j),
            device_id_type=pl.DeviceIdType.MESH,
        )

    def arrival(j):
        return pltpu.make_async_remote_copy(
            src_ref=src.at[j],
            dst_ref=dst.at[j],
            send_sem=send_sem.at[j],
            recv_sem=recv_sem.at[j],
            device_id=partner(j),
            device_id_type=pl.DeviceIdType.MESH,
        )

    def other(j):
        return jnp.logical_or(side != c, slot != j)

    for j in range(peers):

        @pl.when(other(j))
        def _():
            pl.semaphore_signal(
                barrier, inc=1, device_id=partner(j), device_id_type=pl.DeviceIdType.MESH
            )

    @pl.when(side == c)
    def _():
        pl.semaphore_wait(barrier, peers - 1)

    @pl.when(side != c)
    def _():
        pl.semaphore_wait(barrier, peers)

    for j in range(peers):

        @pl.when(other(j))
        def _():
            copy(j).start()

        @pl.when(jnp.logical_not(other(j)))
        def _():
            own = pltpu.make_async_copy(src.at[j], dst.at[j], local_sem)
            own.start()
            own.wait()

    for j in range(peers):

        @pl.when(other(j))
        def _():
            copy(j).wait_send()
            arrival(j).wait_recv()


def scatter_kernel(row_length, width, arrived, source, target, waves, ocean):
    peers = source.shape[0]
    waves[...] = jnp.zeros_like(waves)

    def step(j, carry):
        parts = split_parts(arrived[j])
        hot = block_onehot(source[j], j, row_length, width)
        ocean[j] = join_parts(
            lax.dot_general(parts, hot, NT, preferred_element_type=jnp.float32)
        )
        hot2 = wave_onehot(target[j], waves.shape[1])
        waves[...] += join_parts(
            lax.dot_general(parts, hot2, NT, preferred_element_type=jnp.float32)
        )
        return carry

    lax.fori_loop(0, peers, step, 0)


VMEM = pl.BlockSpec(memory_space=pltpu.VMEM)


def remap(spectra, wave_wet, surface, remap_source, remap_target, remap_weight):
    peers, slots = remap_source.shape[1:]
    span_x, span_y = wave_wet.shape
    rows, cols = surface.shape[1:]
    width = cols // peers
    source = remap_source.reshape(peers, 1, slots)
    target = remap_target.reshape(peers, 1, slots)
    weight = remap_weight.reshape(peers, 1, slots)
    blocks = surface.reshape(3, rows, peers, width).transpose(2, 0, 1, 3).reshape(peers, 3, slots)
    blocks = jnp.concatenate([blocks, jnp.zeros((peers, 5, slots), jnp.float32)], axis=1)
    shape = jax.ShapeDtypeStruct((peers, 8, slots), jnp.float32)
    sent = pl.pallas_call(
        lambda *refs: gather_kernel(cols, width, *refs),
        out_shape=shape,
        in_specs=[VMEM] * 6,
        out_specs=VMEM,
        scratch_shapes=[pltpu.VMEM((8, span_x * span_y), jnp.float32)],
        compiler_params=pltpu.CompilerParams(vmem_limit_bytes=32 * 1024 * 1024),
    )(spectra, wave_wet, blocks, source, target, weight)
    arrived = pl.pallas_call(
        swap_kernel,
        out_shape=shape,
        in_specs=[VMEM],
        out_specs=VMEM,
        scratch_shapes=[
            pltpu.SemaphoreType.DMA((peers,)),
            pltpu.SemaphoreType.DMA((peers,)),
            pltpu.SemaphoreType.DMA,
        ],
        compiler_params=pltpu.CompilerParams(collective_id=0, has_side_effects=True),
    )(sent)
    waves, ocean = pl.pallas_call(
        lambda *refs: scatter_kernel(cols, width, *refs),
        out_shape=(jax.ShapeDtypeStruct((8, span_x * span_y), jnp.float32), shape),
        in_specs=[VMEM] * 3,
        out_specs=(VMEM, VMEM),
        compiler_params=pltpu.CompilerParams(vmem_limit_bytes=32 * 1024 * 1024),
    )(arrived, source, target)
    currents = waves[:3].reshape(3, span_x, span_y)
    ocean_stress = (
        ocean[:, 3:6]
        .reshape(peers, 3, rows, width)
        .transpose(1, 2, 0, 3)
        .reshape(3, rows, cols)
    )
    return currents, ocean_stress


MESH = pl.DeviceIdType.MESH


def enter(t, c, tiles):
    barrier = pltpu.get_barrier_semaphore()
    has_up, has_down = t > 0, t < tiles - 1

    @pl.when(has_up)
    def _():
        pl.semaphore_signal(barrier, inc=1, device_id={"tile": t - 1}, device_id_type=MESH)

    @pl.when(has_down)
    def _():
        pl.semaphore_signal(barrier, inc=1, device_id={"tile": t + 1}, device_id_type=MESH)

    pl.semaphore_signal(barrier, inc=1, device_id={"col": 1 - c}, device_id_type=MESH)

    @pl.when(jnp.logical_and(has_up, has_down))
    def _():
        pl.semaphore_wait(barrier, 3)

    @pl.when(jnp.logical_not(jnp.logical_and(has_up, has_down)))
    def _():
        pl.semaphore_wait(barrier, 2)

    return has_up, has_down


def remote(src, dst, send, recv, **where):
    return pltpu.make_async_remote_copy(
        src_ref=src, dst_ref=dst, send_sem=send, recv_sem=recv, device_id=where, device_id_type=MESH
    )


CHUNKS = 4
UNROLL = 8


def wave_kernel(
    spectra, fields, cosd, sind, speed, freq, out,
    first, last, packed, before, after, beside, f_up, f_down, f_side,
    s_first, s_last, s_pack, r_before, r_after, r_beside, s_field, r_field,
):
    t, c = lax.axis_index("tile"), lax.axis_index("col")
    tiles = lax.axis_size("tile")
    has_up, has_down = enter(t, c, tiles)
    per_chunk = ND // CHUNKS
    chunk_rows = per_chunk * NF
    lane = lax.broadcasted_iota(jnp.int32, (8, 128), 1)
    sub = lax.broadcasted_iota(jnp.int32, (8, 128), 0)
    edge = jnp.where(c == 0, 127, 0)
    is0 = jnp.where(c == 0, 1.0, 0.0)
    is1 = 1.0 - is0

    def field_copies():
        return (
            (has_up, remote(fields, f_down, s_field.at[0], r_field.at[1], tile=t - 1),
             remote(fields, f_up, s_field.at[0], r_field.at[0], tile=t - 1)),
            (has_down, remote(fields, f_up, s_field.at[1], r_field.at[0], tile=t + 1),
             remote(fields, f_down, s_field.at[1], r_field.at[1], tile=t + 1)),
            (None, remote(fields, f_side, s_field.at[2], r_field.at[2], col=1 - c), None),
        )

    def edge_copies(n, q):
        rows = pl.ds(pl.multiple_of(q * chunk_rows, 8), chunk_rows)
        dirs = pl.ds(q * per_chunk, per_chunk)
        up = remote(first.at[n, rows], after.at[n, rows], s_first.at[n, q], r_after.at[n, q], tile=t - 1)
        up_in = remote(first.at[n, rows], before.at[n, rows], s_first.at[n, q], r_before.at[n, q], tile=t - 1)
        down = remote(last.at[n, rows], before.at[n, rows], s_last.at[n, q], r_before.at[n, q], tile=t + 1)
        down_in = remote(last.at[n, rows], after.at[n, rows], s_last.at[n, q], r_after.at[n, q], tile=t + 1)
        side = remote(packed.at[n, dirs], beside.at[n, dirs], s_pack.at[n, q], r_beside.at[n, q], col=1 - c)
        return (has_up, up, up_in), (has_down, down, down_in), (None, side, None)

    def start_all(copies):
        for cond, out_copy, in_copy in copies:
            if cond is None:
                out_copy.start()
            else:
                pl.when(cond)(out_copy.start)

    def wait_all(copies):
        for cond, out_copy, in_copy in copies:
            if cond is None:
                out_copy.wait_send()
                out_copy.wait_recv()
            else:
                pl.when(cond)(out_copy.wait_send)
                pl.when(cond)(in_copy.wait_recv)

    start_all(field_copies())

    @pl.when(jnp.logical_not(has_up))
    def _():
        before[...] = jnp.zeros_like(before)
        f_up[...] = jnp.zeros_like(f_up)

    @pl.when(jnp.logical_not(has_down))
    def _():
        after[...] = jnp.zeros_like(after)
        f_down[...] = jnp.zeros_like(f_down)

    drift_x, drift_y, wet = fields[0], fields[1], fields[2]
    wind_x, wind_y, level = fields[3], fields[4], fields[5]
    calm = 0.3 * jnp.exp(-0.5 * level) * (1.0 / (ND * NF))

    def keep_edges(n, d, base, i, f, value, pack):
        first[n, pl.ds(base + i, 1), :] = value[0:1, :]
        last[n, pl.ds(base + i, 1), :] = value[7:8, :]
        shift = lax.rem(f + 256 - edge, 128)
        return jnp.where(lane == f, pltpu.roll(value, shift, 1), pack)

    def opening(q, total):
        def one(dd, total):
            d = q * per_chunk + dd

            def group(fg, carry):
                total, pack = carry
                base = pl.multiple_of(d * NF + fg * UNROLL, UNROLL)
                for i in range(UNROLL):
                    value = spectra[base + i] * wet
                    out[base + i] = value
                    total = total + value
                    pack = keep_edges(0, d, base, i, fg * UNROLL + i, value, pack)
                return total, pack

            total, pack = lax.fori_loop(
                0, NF // UNROLL, group, (total, jnp.zeros((8, 128), jnp.float32))
            )
            packed[0, d] = pack
            return total

        total = lax.fori_loop(0, per_chunk, one, total)
        start_all(edge_copies(0, q))
        return total

    total = lax.fori_loop(0, CHUNKS, opening, jnp.zeros((8, 128), jnp.float32))
    wait_all(field_copies())

    def row_before(i):
        return jnp.where(sub == 0, f_up[i][7:8], pltpu.roll(fields[i], 1, 0))

    def row_after(i):
        return jnp.where(sub == 7, f_down[i][0:1], pltpu.roll(fields[i], 7, 0))

    def lane_before(i):
        return jnp.where(lane == 0, pltpu.roll(f_side[i], 1, 1) * is1, pltpu.roll(fields[i], 1, 1))

    def lane_after(i):
        return jnp.where(
            lane == 127, pltpu.roll(f_side[i], 127, 1) * is0, pltpu.roll(fields[i], 127, 1)
        )

    faces = []
    for get, i in ((row_before, 0), (row_after, 0), (lane_before, 1), (lane_after, 1)):
        door = wet * get(2)
        faces.append((door, door * 0.5 * (fields[i] + get(i))))
    low_mask = jnp.logical_and(lane == 0, c == 1)
    high_mask = jnp.logical_and(lane == 127, c == 0)

    def column(i):
        return jnp.sum(
            jnp.where(lane == 127 - edge, f_side[i], 0.0), axis=1, keepdims=True
        ) + jnp.zeros((8, 128), jnp.float32)

    side_x, side_y, side_level = column(3), column(4), column(5)
    side_calm = 0.3 * jnp.exp(-0.5 * side_level) * (1.0 / (ND * NF))
    lane_freq = jnp.where(lane < NF, (lane + 1).astype(jnp.float32) * (2.0 / NF), 0.0)
    freq_column = (
        lax.broadcasted_iota(jnp.int32, (NF, 128), 0) + 1
    ).astype(jnp.float32) * (2.0 / NF)
    rows_of = (
        (before, f_up[3][7:8], f_up[4][7:8], 0.3 * jnp.exp(-0.5 * f_up[5][7:8]) * (1.0 / (ND * NF))),
        (after, f_down[3][0:1], f_down[4][0:1], 0.3 * jnp.exp(-0.5 * f_down[5][0:1]) * (1.0 / (ND * NF))),
    )

    def step(n, total):
        def arrive(q, carry):
            wait_all(edge_copies(n, q))
            return carry

        lax.fori_loop(0, CHUNKS, arrive, 0)

        def add(d, carry):
            rows = pl.ds(pl.multiple_of(d * NF, NF), NF)
            return carry[0] + before[n, rows], carry[1] + after[n, rows], carry[2] + beside[n, d]

        zero = jnp.zeros((NF, 128), jnp.float32)
        sums = lax.fori_loop(0, ND, add, (zero, zero, jnp.zeros((8, 128), jnp.float32)))
        fades = [jnp.sum(sums[i], axis=0, keepdims=True) * rows_of[i][3] for i in range(2)]
        side_fade = jnp.sum(sums[2], axis=1, keepdims=True) * side_calm
        fade = total * calm

        def one(d, total):
            cos, sin = cosd[d], sind[d]
            rows = pl.ds(pl.multiple_of(d * NF, NF), NF)
            for i in range(2):
                ref, wx, wy, _ = rows_of[i]
                push = 0.02 * jnp.maximum(wx * cos + wy * sin, 0.0)
                ref[n, rows] = ref[n, rows] * jnp.exp(push * freq_column - fades[i])
            push = 0.02 * jnp.maximum(side_x * cos + side_y * sin, 0.0)
            side = beside[n, d] * jnp.exp(push * lane_freq - side_fade)
            push = 0.02 * jnp.maximum(wind_x * cos + wind_y * sin, 0.0)

            def group(fg, carry):
                total, pack = carry
                base = pl.multiple_of(d * NF + fg * UNROLL, UNROLL)
                up8 = before[n, pl.ds(base, UNROLL)]
                down8 = after[n, pl.ds(base, UNROLL)]
                for i in range(UNROLL):
                    f = fg * UNROLL + i
                    e = out[base + i] * jnp.exp(push * freq[f] - fade)
                    vx, vy = speed[f] * cos, speed[f] * sin
                    halo = pltpu.roll(side, lax.rem(edge + 128 - f, 128), 1)
                    x0 = jnp.where(sub == 0, up8[i : i + 1], pltpu.roll(e, 1, 0))
                    x1 = jnp.where(sub == 7, down8[i : i + 1], pltpu.roll(e, 7, 0))
                    y0 = jnp.where(low_mask, halo, pltpu.roll(e, 1, 1))
                    y1 = jnp.where(high_mask, halo, pltpu.roll(e, 127, 1))
                    wx0 = vx * faces[0][0] + faces[0][1]
                    wx1 = vx * faces[1][0] + faces[1][1]
                    wy0 = vy * faces[2][0] + faces[2][1]
                    wy1 = vy * faces[3][0] + faces[3][1]
                    fx1 = jnp.maximum(wx1, 0.0) * e + jnp.minimum(wx1, 0.0) * x1
                    fx0 = jnp.maximum(wx0, 0.0) * x0 + jnp.minimum(wx0, 0.0) * e
                    fy1 = jnp.maximum(wy1, 0.0) * e + jnp.minimum(wy1, 0.0) * y1
                    fy0 = jnp.maximum(wy0, 0.0) * y0 + jnp.minimum(wy0, 0.0) * e
                    value = e - (fx1 - fx0) - (fy1 - fy0)
                    out[base + i] = value
                    total = total + value
                    pack = keep_edges(n + 1, d, base, i, f, value, pack)
                return total, pack

            total, pack = lax.fori_loop(
                0, NF // UNROLL, group, (total, jnp.zeros((8, 128), jnp.float32))
            )
            packed[n + 1, d] = pack
            return total

        def chunk(q, total):
            total = lax.fori_loop(q * per_chunk, (q + 1) * per_chunk, one, total)

            @pl.when(n < WSTEPS - 1)
            def _():
                start_all(edge_copies(n + 1, q))

            return total

        return lax.fori_loop(0, CHUNKS, chunk, jnp.zeros((8, 128), jnp.float32))

    lax.fori_loop(0, WSTEPS, step, total)


def wave_steps(spectra, fields, tables):
    _, _, span_x, span_y = spectra.shape
    bins = ND * NF
    smem = pl.BlockSpec(memory_space=pltpu.SMEM)
    dma = pltpu.SemaphoreType.DMA
    f32 = jnp.float32
    sems = [dma((WSTEPS, CHUNKS))] * 6 + [dma((3,))] * 2
    result = pl.pallas_call(
        wave_kernel,
        out_shape=jax.ShapeDtypeStruct((bins, span_x, span_y), f32),
        in_specs=[VMEM, VMEM, smem, smem, smem, smem],
        out_specs=VMEM,
        scratch_shapes=[
            pltpu.VMEM((WSTEPS + 1, bins, span_y), f32),
            pltpu.VMEM((WSTEPS + 1, bins, span_y), f32),
            pltpu.VMEM((WSTEPS + 1, ND, span_x, span_y), f32),
            pltpu.VMEM((WSTEPS, bins, span_y), f32),
            pltpu.VMEM((WSTEPS, bins, span_y), f32),
            pltpu.VMEM((WSTEPS, ND, span_x, span_y), f32),
            pltpu.VMEM((6, span_x, span_y), f32),
            pltpu.VMEM((6, span_x, span_y), f32),
            pltpu.VMEM((6, span_x, span_y), f32),
        ]
        + sems,
        compiler_params=pltpu.CompilerParams(
            collective_id=1, has_side_effects=True, vmem_limit_bytes=48 * 1024 * 1024
        ),
    )(spectra.reshape(bins, span_x, span_y), fields, *tables)
    return result.reshape(ND, NF, span_x, span_y)


def ocean_kernel(
    zonal, meridional, height, stress, sea_in, coriolis_in, thick, inverse, mixing,
    out_z, out_m, out_h, plane, other, s_up, s_down, r_up, r_down, s_side, r_side,
):
    t, c = lax.axis_index("tile"), lax.axis_index("col")
    tiles = lax.axis_size("tile")
    levels, rows, cols = zonal.shape
    has_up, has_down = enter(t, c, tiles)
    sea = sea_in[...].astype(jnp.float32)
    coriolis = coriolis_in[...]
    own = slice(8, 8 + rows)
    wide = rows + 16
    lane = lax.broadcasted_iota(jnp.int32, (wide, cols), 1)
    line = lax.broadcasted_iota(jnp.int32, (wide, cols), 0)
    first_row = jnp.where(has_up, 0, 8)
    end_row = jnp.where(has_down, wide, 8 + rows)
    inside = jnp.where(jnp.logical_and(line >= first_row, line < end_row), 1.0, 0.0)
    is0 = jnp.where(c == 0, 1.0, 0.0)
    is1 = 1.0 - is0

    @pl.when(jnp.logical_not(has_up))
    def _():
        plane[:, :, 0:8, :] = jnp.zeros((OSTEPS, 6, 8, cols), jnp.float32)

    @pl.when(jnp.logical_not(has_down))
    def _():
        plane[:, :, 8 + rows : wide, :] = jnp.zeros((OSTEPS, 6, 8, cols), jnp.float32)

    def dx(value, beside, left, right):
        ahead = jnp.where(lane == cols - 1, pltpu.roll(beside, cols - 1, 1) * right, pltpu.roll(value, cols - 1, 1))
        back = jnp.where(lane == 0, pltpu.roll(beside, 1, 1) * left, pltpu.roll(value, 1, 1))
        return 0.5 * (ahead - back)

    def dy(value):
        return 0.5 * (pltpu.roll(value, wide - 1, 0) - pltpu.roll(value, 1, 0))

    zero = jnp.zeros((rows, cols), jnp.float32)

    def load(k, carry):
        z, m = zonal[k] * sea, meridional[k] * sea
        out_z[k] = z
        out_m[k] = m
        return carry[0] + thick[k] * z, carry[1] + thick[k] * m, carry[2] + thick[k]

    tx, ty, depth = lax.fori_loop(0, levels, load, (zero, zero, zero))
    now = height[...]
    force_x = force_y = zero
    for n in range(OSTEPS):
        plane[n, 0, own, :] = tx / depth
        plane[n, 1, own, :] = ty / depth
        plane[n, 2, own, :] = now
        count = 6 if n == 0 else 3
        if n == 0:
            for i in range(3):
                plane[n, 3 + i, own, :] = stress[i]
        part = pl.ds(0, count)
        top, bottom = pl.ds(8, 8), pl.ds(rows, 8)
        head, tail = pl.ds(0, 8), pl.ds(8 + rows, 8)
        up = remote(plane.at[n, part, top], plane.at[n, part, tail], s_up.at[n], r_down.at[n], tile=t - 1)
        up_in = remote(plane.at[n, part, top], plane.at[n, part, head], s_up.at[n], r_up.at[n], tile=t - 1)
        down = remote(plane.at[n, part, bottom], plane.at[n, part, head], s_down.at[n], r_up.at[n], tile=t + 1)
        down_in = remote(plane.at[n, part, bottom], plane.at[n, part, tail], s_down.at[n], r_down.at[n], tile=t + 1)
        pl.when(has_up)(up.start)
        pl.when(has_down)(down.start)
        pl.when(has_up)(up.wait_send)
        pl.when(has_up)(up_in.wait_recv)
        pl.when(has_down)(down.wait_send)
        pl.when(has_down)(down_in.wait_recv)
        side = remote(plane.at[n, part], other.at[n, part], s_side.at[n], r_side.at[n], col=1 - c)
        side.start()
        side.wait_send()
        side.wait_recv()
        mine = [plane[n, i] for i in range(count)]
        near = [other[n, i] for i in range(count)]
        if n == 0:
            slope = [dx(mine[3 + i], near[3 + i], is1, is0) for i in range(2)]
            force_x = (-0.5 * (slope[0] + dy(mine[4])))[own]
            force_y = (-0.5 * (slope[1] + dy(mine[5])))[own]
        high = (mine[2] - 0.2 * (dx(mine[0], near[0], is1, is0) + dy(mine[1]))) * inside
        high_near = (near[2] - 0.2 * (dx(near[0], mine[0], is0, is1) + dy(near[1]))) * inside
        press_x = (0.2 * dx(high, high_near, is1, is0))[own]
        press_y = (0.2 * dy(high))[own]
        now = high[own]

        def level(k, carry):
            tx, ty, flux_z, flux_m, z, m = carry
            z_next, m_next = out_z[k + 1], out_m[k + 1]
            low_z = mixing[k + 1] * (z - z_next)
            low_m = mixing[k + 1] * (m - m_next)
            new_z = (z + coriolis * m - press_x + (flux_z - low_z) * inverse[k]) * sea
            new_m = (m - coriolis * z - press_y + (flux_m - low_m) * inverse[k]) * sea
            out_z[k] = new_z
            out_m[k] = new_m
            return tx + thick[k] * new_z, ty + thick[k] * new_m, low_z, low_m, z_next, m_next

        tx, ty, flux_z, flux_m, z, m = lax.fori_loop(
            0, levels - 1, level, (zero, zero, force_x, force_y, out_z[0], out_m[0])
        )
        k = levels - 1
        new_z = (z + coriolis * m - press_x + (flux_z - mixing[0] * z) * inverse[k]) * sea
        new_m = (m - coriolis * z - press_y + (flux_m - mixing[0] * m) * inverse[k]) * sea
        out_z[k] = new_z
        out_m[k] = new_m
        tx, ty = tx + thick[k] * new_z, ty + thick[k] * new_m
    out_h[...] = now


def ocean_steps(zonal, meridional, height, stress, sea, coriolis, thickness, mixing):
    rows, cols = height.shape
    smem = pl.BlockSpec(memory_space=pltpu.SMEM)
    f32 = jnp.float32
    flow = jax.ShapeDtypeStruct(zonal.shape, f32)
    return pl.pallas_call(
        ocean_kernel,
        out_shape=(flow, flow, jax.ShapeDtypeStruct(height.shape, f32)),
        in_specs=[VMEM] * 6 + [smem] * 3,
        out_specs=(VMEM, VMEM, VMEM),
        scratch_shapes=[pltpu.VMEM((OSTEPS, 6, rows + 16, cols), f32)] * 2
        + [pltpu.SemaphoreType.DMA((OSTEPS,))] * 6,
        compiler_params=pltpu.CompilerParams(
            collective_id=2, has_side_effects=True, vmem_limit_bytes=32 * 1024 * 1024
        ),
    )(zonal, meridional, height, stress, sea, coriolis, thickness, 1.0 / thickness, mixing)


def body(
    zonal_velocity,
    meridional_velocity,
    surface_height,
    thickness,
    mixing,
    ocean_wet,
    spectra,
    wind_speed,
    wind_direction,
    wave_wet,
    remap_source,
    remap_target,
    remap_weight,
):
    tables = spectral_tables()
    rows, cols = surface_height.shape
    total_rows = rows * lax.axis_size("tile")
    sea_cells = ocean_wet.astype(jnp.float32)
    wet_cells = wave_wet.astype(jnp.float32)
    surface = jnp.stack(
        [zonal_velocity[0] * sea_cells, meridional_velocity[0] * sea_cells, surface_height]
    )
    currents, ocean_stress = remap(
        spectra, wave_wet, surface, remap_source, remap_target, remap_weight
    )
    fields = jnp.stack(
        [
            0.03 * currents[0],
            0.03 * currents[1],
            wet_cells,
            wind_speed * jnp.cos(wind_direction),
            wind_speed * jnp.sin(wind_direction),
            currents[2],
        ]
    )
    energy = wave_steps(spectra, fields, tables)
    row_start = lax.axis_index("tile") * rows
    coriolis = (
        0.1 + 0.1 * ((row_start + jnp.arange(rows)).astype(jnp.float32) + 0.5) / total_rows
    )[:, None] + jnp.zeros((rows, cols), jnp.float32)
    zonal, meridional, height = ocean_steps(
        zonal_velocity, meridional_velocity, surface_height, ocean_stress, ocean_wet, coriolis,
        thickness, mixing,
    )
    return (zonal, meridional, height, energy)


def solution(mesh):
    return jax.shard_map(
        body,
        mesh=mesh,
        in_specs=(
            P(None, ("groups", "tile"), "col"),
            P(None, ("groups", "tile"), "col"),
            P(("groups", "tile"), "col"),
            P(),
            P(),
            P(("groups", "tile"), "col"),
            P(None, None, ("groups", "tile"), "col"),
            P(("groups", "tile"), "col"),
            P(("groups", "tile"), "col"),
            P(("groups", "tile"), "col"),
            P(("groups", "tile", "col"), None, None),
            P(("groups", "tile", "col"), None, None),
            P(("groups", "tile", "col"), None, None),
        ),
        out_specs=(
            P(None, ("groups", "tile"), "col"),
            P(None, ("groups", "tile"), "col"),
            P(("groups", "tile"), "col"),
            P(None, None, ("groups", "tile"), "col"),
        ),
        check_vma=False,
    )
```

```python
import math

import jax
import jax.numpy as jnp
from jax import lax
from jax.experimental import pallas as pl
from jax.experimental.pallas import tpu as pltpu
from jax.sharding import PartitionSpec as P

ND = 36
NF = 32
WSTEPS = 4
OSTEPS = 4


def spectral_tables():
    angles = (jnp.arange(ND, dtype=jnp.float32) + 0.5) * (2.0 * math.pi / ND)
    group_speed = 0.5 * jnp.power(jnp.float32(1.1), -jnp.arange(NF, dtype=jnp.float32))
    freq_weight = 2.0 * (jnp.arange(NF, dtype=jnp.float32) + 1.0) / NF
    return (jnp.cos(angles), jnp.sin(angles), group_speed, freq_weight)


def split_parts(x):
    high = x.astype(jnp.bfloat16).astype(jnp.float32)
    rest = x - high
    middle = rest.astype(jnp.bfloat16).astype(jnp.float32)
    low = rest - middle
    return jnp.concatenate([high, middle, low], axis=0).astype(jnp.bfloat16)


def join_parts(r):
    return r[0:8] + r[8:16] + r[16:24]


def block_onehot(source_row, j, row_length, width):
    cells = source_row.shape[1]
    n = lax.broadcasted_iota(jnp.int32, (cells, cells), 0)
    ids = (n // width) * row_length + j * width + n % width
    return jnp.where(ids == source_row, 1.0, 0.0).astype(jnp.bfloat16)


def wave_onehot(target_row, cells):
    n = lax.broadcasted_iota(jnp.int32, (cells, target_row.shape[1]), 0)
    return jnp.where(n == target_row, 1.0, 0.0).astype(jnp.bfloat16)


NN = (((1,), (0,)), ((), ()))
NT = (((1,), (1,)), ((), ()))


def gather_kernel(row_length, width, spectra, wet, surface, source, target, weight, out, flat):
    span_x, span_y = wet.shape
    peers = source.shape[0]
    zero = jnp.zeros((span_x, span_y), jnp.float32)
    acc = [zero, zero, zero]
    for d in range(ND):
        theta = (d + 0.5) * (2.0 * math.pi / ND)
        part = jnp.sum(spectra[d], axis=0)
        cos, sin = math.cos(theta), math.sin(theta)
        for c, m in enumerate((cos * cos, cos * sin, sin * sin)):
            acc[c] = acc[c] + part * (m * 0.5 / (ND * NF))
    wetf = wet[...].astype(jnp.float32)
    flat[...] = jnp.zeros_like(flat)
    for c in range(3):
        plane = acc[c] * wetf
        for x in range(span_x):
            flat[3 + c : 4 + c, x * span_y : (x + 1) * span_y] = plane[x : x + 1, :]
    stress = split_parts(flat[...])

    def step(j, carry):
        hot = block_onehot(source[j], j, row_length, width)
        values = join_parts(
            lax.dot_general(split_parts(surface[j]), hot, NN, preferred_element_type=jnp.float32)
        )
        hot2 = wave_onehot(target[j], span_x * span_y)
        back = join_parts(
            lax.dot_general(stress, hot2, NN, preferred_element_type=jnp.float32)
        )
        out[j] = values * weight[j] + back
        return carry

    lax.fori_loop(0, peers, step, 0)


def swap_kernel(src, dst, send_sem, recv_sem, local_sem):
    peers = src.shape[0]
    t = lax.axis_index("tile")
    c = lax.axis_index("col")
    side = t // peers
    slot = lax.rem(t, peers)
    barrier = pltpu.get_barrier_semaphore()

    def partner(j):
        return {"tile": c * peers + j, "col": side}

    def copy(j):
        return pltpu.make_async_remote_copy(
            src_ref=src.at[j],
            dst_ref=dst.at[slot],
            send_sem=send_sem.at[j],
            recv_sem=recv_sem.at[slot],
            device_id=partner(j),
            device_id_type=pl.DeviceIdType.MESH,
        )

    def arrival(j):
        return pltpu.make_async_remote_copy(
            src_ref=src.at[j],
            dst_ref=dst.at[j],
            send_sem=send_sem.at[j],
            recv_sem=recv_sem.at[j],
            device_id=partner(j),
            device_id_type=pl.DeviceIdType.MESH,
        )

    def other(j):
        return jnp.logical_or(side != c, slot != j)

    for j in range(peers):

        @pl.when(other(j))
        def _():
            pl.semaphore_signal(
                barrier, inc=1, device_id=partner(j), device_id_type=pl.DeviceIdType.MESH
            )

    @pl.when(side == c)
    def _():
        pl.semaphore_wait(barrier, peers - 1)

    @pl.when(side != c)
    def _():
        pl.semaphore_wait(barrier, peers)

    for j in range(peers):

        @pl.when(other(j))
        def _():
            copy(j).start()

        @pl.when(jnp.logical_not(other(j)))
        def _():
            own = pltpu.make_async_copy(src.at[j], dst.at[j], local_sem)
            own.start()
            own.wait()

    for j in range(peers):

        @pl.when(other(j))
        def _():
            copy(j).wait_send()
            arrival(j).wait_recv()


def scatter_kernel(row_length, width, arrived, source, target, waves, ocean):
    peers = source.shape[0]
    waves[...] = jnp.zeros_like(waves)

    def step(j, carry):
        parts = split_parts(arrived[j])
        hot = block_onehot(source[j], j, row_length, width)
        ocean[j] = join_parts(
            lax.dot_general(parts, hot, NT, preferred_element_type=jnp.float32)
        )
        hot2 = wave_onehot(target[j], waves.shape[1])
        waves[...] += join_parts(
            lax.dot_general(parts, hot2, NT, preferred_element_type=jnp.float32)
        )
        return carry

    lax.fori_loop(0, peers, step, 0)


VMEM = pl.BlockSpec(memory_space=pltpu.VMEM)


def remap(spectra, wave_wet, surface, remap_source, remap_target, remap_weight):
    peers, slots = remap_source.shape[1:]
    span_x, span_y = wave_wet.shape
    rows, cols = surface.shape[1:]
    width = cols // peers
    source = remap_source.reshape(peers, 1, slots)
    target = remap_target.reshape(peers, 1, slots)
    weight = remap_weight.reshape(peers, 1, slots)
    blocks = surface.reshape(3, rows, peers, width).transpose(2, 0, 1, 3).reshape(peers, 3, slots)
    blocks = jnp.concatenate([blocks, jnp.zeros((peers, 5, slots), jnp.float32)], axis=1)
    shape = jax.ShapeDtypeStruct((peers, 8, slots), jnp.float32)
    sent = pl.pallas_call(
        lambda *refs: gather_kernel(cols, width, *refs),
        out_shape=shape,
        in_specs=[VMEM] * 6,
        out_specs=VMEM,
        scratch_shapes=[pltpu.VMEM((8, span_x * span_y), jnp.float32)],
        compiler_params=pltpu.CompilerParams(vmem_limit_bytes=32 * 1024 * 1024),
    )(spectra, wave_wet, blocks, source, target, weight)
    arrived = pl.pallas_call(
        swap_kernel,
        out_shape=shape,
        in_specs=[VMEM],
        out_specs=VMEM,
        scratch_shapes=[
            pltpu.SemaphoreType.DMA((peers,)),
            pltpu.SemaphoreType.DMA((peers,)),
            pltpu.SemaphoreType.DMA,
        ],
        compiler_params=pltpu.CompilerParams(collective_id=0, has_side_effects=True),
    )(sent)
    waves, ocean = pl.pallas_call(
        lambda *refs: scatter_kernel(cols, width, *refs),
        out_shape=(jax.ShapeDtypeStruct((8, span_x * span_y), jnp.float32), shape),
        in_specs=[VMEM] * 3,
        out_specs=(VMEM, VMEM),
        compiler_params=pltpu.CompilerParams(vmem_limit_bytes=32 * 1024 * 1024),
    )(arrived, source, target)
    currents = waves[:3].reshape(3, span_x, span_y)
    ocean_stress = (
        ocean[:, 3:6]
        .reshape(peers, 3, rows, width)
        .transpose(1, 2, 0, 3)
        .reshape(3, rows, cols)
    )
    return currents, ocean_stress


MESH = pl.DeviceIdType.MESH


def enter(t, c, tiles):
    barrier = pltpu.get_barrier_semaphore()
    has_up, has_down = t > 0, t < tiles - 1

    @pl.when(has_up)
    def _():
        pl.semaphore_signal(barrier, inc=1, device_id={"tile": t - 1}, device_id_type=MESH)

    @pl.when(has_down)
    def _():
        pl.semaphore_signal(barrier, inc=1, device_id={"tile": t + 1}, device_id_type=MESH)

    pl.semaphore_signal(barrier, inc=1, device_id={"col": 1 - c}, device_id_type=MESH)

    @pl.when(jnp.logical_and(has_up, has_down))
    def _():
        pl.semaphore_wait(barrier, 3)

    @pl.when(jnp.logical_not(jnp.logical_and(has_up, has_down)))
    def _():
        pl.semaphore_wait(barrier, 2)

    return has_up, has_down


def remote(src, dst, send, recv, **where):
    return pltpu.make_async_remote_copy(
        src_ref=src, dst_ref=dst, send_sem=send, recv_sem=recv, device_id=where, device_id_type=MESH
    )


CHUNKS = 4
UNROLL = 32
LEVELS = 7


def wave_kernel(
    spectra, fields, cosd, sind, speed, freq, out,
    first, last, packed, before, after, beside, f_up, f_down, f_side,
    s_first, s_last, s_pack, r_before, r_after, r_beside, s_field, r_field,
):
    t, c = lax.axis_index("tile"), lax.axis_index("col")
    tiles = lax.axis_size("tile")
    has_up, has_down = enter(t, c, tiles)
    per_chunk = ND // CHUNKS
    chunk_rows = per_chunk * NF
    lane = lax.broadcasted_iota(jnp.int32, (8, 128), 1)
    sub = lax.broadcasted_iota(jnp.int32, (8, 128), 0)
    edge = jnp.where(c == 0, 127, 0)
    is0 = jnp.where(c == 0, 1.0, 0.0)
    is1 = 1.0 - is0

    def field_copies():
        return (
            (has_up, remote(fields, f_down, s_field.at[0], r_field.at[1], tile=t - 1),
             remote(fields, f_up, s_field.at[0], r_field.at[0], tile=t - 1)),
            (has_down, remote(fields, f_up, s_field.at[1], r_field.at[0], tile=t + 1),
             remote(fields, f_down, s_field.at[1], r_field.at[1], tile=t + 1)),
            (None, remote(fields, f_side, s_field.at[2], r_field.at[2], col=1 - c), None),
        )

    def edge_copies(n, q):
        rows = pl.ds(pl.multiple_of(q * chunk_rows, 8), chunk_rows)
        dirs = pl.ds(q * per_chunk, per_chunk)
        up = remote(first.at[n, rows], after.at[n, rows], s_first.at[n, q], r_after.at[n, q], tile=t - 1)
        up_in = remote(first.at[n, rows], before.at[n, rows], s_first.at[n, q], r_before.at[n, q], tile=t - 1)
        down = remote(last.at[n, rows], before.at[n, rows], s_last.at[n, q], r_before.at[n, q], tile=t + 1)
        down_in = remote(last.at[n, rows], after.at[n, rows], s_last.at[n, q], r_after.at[n, q], tile=t + 1)
        side = remote(packed.at[n, dirs], beside.at[n, dirs], s_pack.at[n, q], r_beside.at[n, q], col=1 - c)
        return (has_up, up, up_in), (has_down, down, down_in), (None, side, None)

    def start_all(copies):
        for cond, out_copy, in_copy in copies:
            if cond is None:
                out_copy.start()
            else:
                pl.when(cond)(out_copy.start)

    def wait_all(copies):
        for cond, out_copy, in_copy in copies:
            if cond is None:
                out_copy.wait_send()
                out_copy.wait_recv()
            else:
                pl.when(cond)(out_copy.wait_send)
                pl.when(cond)(in_copy.wait_recv)

    start_all(field_copies())

    @pl.when(jnp.logical_not(has_up))
    def _():
        before[...] = jnp.zeros_like(before)
        f_up[...] = jnp.zeros_like(f_up)

    @pl.when(jnp.logical_not(has_down))
    def _():
        after[...] = jnp.zeros_like(after)
        f_down[...] = jnp.zeros_like(f_down)

    drift_x, drift_y, wet = fields[0], fields[1], fields[2]
    wind_x, wind_y, level = fields[3], fields[4], fields[5]
    calm = 0.3 * jnp.exp(-0.5 * level) * (1.0 / (ND * NF))

    def keep_edges(n, d, base, i, f, value, pack):
        first[n, pl.ds(base + i, 1), :] = value[0:1, :]
        last[n, pl.ds(base + i, 1), :] = value[7:8, :]
        shift = lax.rem(f + 256 - edge, 128)
        return jnp.where(lane == f, pltpu.roll(value, shift, 1), pack)

    def opening(q, total):
        def one(dd, total):
            d = q * per_chunk + dd

            def group(fg, carry):
                total, pack = carry
                base = pl.multiple_of(d * NF + fg * UNROLL, UNROLL)
                for i in range(UNROLL):
                    value = spectra[base + i] * wet
                    out[base + i] = value
                    total = total + value
                    pack = keep_edges(0, d, base, i, fg * UNROLL + i, value, pack)
                return total, pack

            total, pack = lax.fori_loop(
                0, NF // UNROLL, group, (total, jnp.zeros((8, 128), jnp.float32))
            )
            packed[0, d] = pack
            return total

        total = lax.fori_loop(0, per_chunk, one, total)
        start_all(edge_copies(0, q))
        return total

    total = lax.fori_loop(0, CHUNKS, opening, jnp.zeros((8, 128), jnp.float32))
    wait_all(field_copies())

    def row_before(i):
        return jnp.where(sub == 0, f_up[i][7:8], pltpu.roll(fields[i], 1, 0))

    def row_after(i):
        return jnp.where(sub == 7, f_down[i][0:1], pltpu.roll(fields[i], 7, 0))

    def lane_before(i):
        return jnp.where(lane == 0, pltpu.roll(f_side[i], 1, 1) * is1, pltpu.roll(fields[i], 1, 1))

    def lane_after(i):
        return jnp.where(
            lane == 127, pltpu.roll(f_side[i], 127, 1) * is0, pltpu.roll(fields[i], 127, 1)
        )

    faces = []
    for get, i in ((row_before, 0), (row_after, 0), (lane_before, 1), (lane_after, 1)):
        door = wet * get(2)
        faces.append((door, door * 0.5 * (fields[i] + get(i))))
    low_mask = jnp.logical_and(lane == 0, c == 1)
    high_mask = jnp.logical_and(lane == 127, c == 0)

    def column(i):
        return jnp.sum(
            jnp.where(lane == 127 - edge, f_side[i], 0.0), axis=1, keepdims=True
        ) + jnp.zeros((8, 128), jnp.float32)

    side_x, side_y, side_level = column(3), column(4), column(5)
    side_calm = 0.3 * jnp.exp(-0.5 * side_level) * (1.0 / (ND * NF))
    lane_freq = jnp.where(lane < NF, (lane + 1).astype(jnp.float32) * (2.0 / NF), 0.0)
    freq_column = (
        lax.broadcasted_iota(jnp.int32, (NF, 128), 0) + 1
    ).astype(jnp.float32) * (2.0 / NF)
    rows_of = (
        (before, f_up[3][7:8], f_up[4][7:8], 0.3 * jnp.exp(-0.5 * f_up[5][7:8]) * (1.0 / (ND * NF))),
        (after, f_down[3][0:1], f_down[4][0:1], 0.3 * jnp.exp(-0.5 * f_down[5][0:1]) * (1.0 / (ND * NF))),
    )

    def step(n, total):
        def arrive(q, carry):
            wait_all(edge_copies(n, q))
            return carry

        lax.fori_loop(0, CHUNKS, arrive, 0)

        def add(d, carry):
            rows = pl.ds(pl.multiple_of(d * NF, NF), NF)
            return carry[0] + before[n, rows], carry[1] + after[n, rows], carry[2] + beside[n, d]

        zero = jnp.zeros((NF, 128), jnp.float32)
        sums = lax.fori_loop(0, ND, add, (zero, zero, jnp.zeros((8, 128), jnp.float32)))
        fades = [jnp.sum(sums[i], axis=0, keepdims=True) * rows_of[i][3] for i in range(2)]
        side_fade = jnp.sum(sums[2], axis=1, keepdims=True) * side_calm
        fade = total * calm

        def one(d, total):
            cos, sin = cosd[d], sind[d]
            rows = pl.ds(pl.multiple_of(d * NF, NF), NF)
            for i in range(2):
                ref, wx, wy, _ = rows_of[i]
                push = 0.02 * jnp.maximum(wx * cos + wy * sin, 0.0)
                ref[n, rows] = ref[n, rows] * jnp.exp(push * freq_column - fades[i])
            push = 0.02 * jnp.maximum(side_x * cos + side_y * sin, 0.0)
            side = beside[n, d] * jnp.exp(push * lane_freq - side_fade)
            push = 0.02 * jnp.maximum(wind_x * cos + wind_y * sin, 0.0)

            def group(fg, carry):
                total, pack = carry
                base = pl.multiple_of(d * NF + fg * UNROLL, UNROLL)
                up8 = before[n, pl.ds(base, UNROLL)]
                down8 = after[n, pl.ds(base, UNROLL)]
                for i in range(UNROLL):
                    f = fg * UNROLL + i
                    e = out[base + i] * jnp.exp(push * freq[f] - fade)
                    vx, vy = speed[f] * cos, speed[f] * sin
                    halo = pltpu.roll(side, lax.rem(edge + 128 - f, 128), 1)
                    x0 = jnp.where(sub == 0, up8[i : i + 1], pltpu.roll(e, 1, 0))
                    x1 = jnp.where(sub == 7, down8[i : i + 1], pltpu.roll(e, 7, 0))
                    y0 = jnp.where(low_mask, halo, pltpu.roll(e, 1, 1))
                    y1 = jnp.where(high_mask, halo, pltpu.roll(e, 127, 1))
                    wx0 = vx * faces[0][0] + faces[0][1]
                    wx1 = vx * faces[1][0] + faces[1][1]
                    wy0 = vy * faces[2][0] + faces[2][1]
                    wy1 = vy * faces[3][0] + faces[3][1]
                    fx1 = jnp.maximum(wx1, 0.0) * e + jnp.minimum(wx1, 0.0) * x1
                    fx0 = jnp.maximum(wx0, 0.0) * x0 + jnp.minimum(wx0, 0.0) * e
                    fy1 = jnp.maximum(wy1, 0.0) * e + jnp.minimum(wy1, 0.0) * y1
                    fy0 = jnp.maximum(wy0, 0.0) * y0 + jnp.minimum(wy0, 0.0) * e
                    value = e - (fx1 - fx0) - (fy1 - fy0)
                    out[base + i] = value
                    total = total + value
                    pack = keep_edges(n + 1, d, base, i, f, value, pack)
                return total, pack

            total, pack = lax.fori_loop(
                0, NF // UNROLL, group, (total, jnp.zeros((8, 128), jnp.float32))
            )
            packed[n + 1, d] = pack
            return total

        def chunk(q, total):
            total = lax.fori_loop(q * per_chunk, (q + 1) * per_chunk, one, total)

            @pl.when(n < WSTEPS - 1)
            def _():
                start_all(edge_copies(n + 1, q))

            return total

        return lax.fori_loop(0, CHUNKS, chunk, jnp.zeros((8, 128), jnp.float32))

    lax.fori_loop(0, WSTEPS, step, total)


def wave_steps(spectra, fields, tables):
    _, _, span_x, span_y = spectra.shape
    bins = ND * NF
    smem = pl.BlockSpec(memory_space=pltpu.SMEM)
    dma = pltpu.SemaphoreType.DMA
    f32 = jnp.float32
    sems = [dma((WSTEPS, CHUNKS))] * 6 + [dma((3,))] * 2
    result = pl.pallas_call(
        wave_kernel,
        out_shape=jax.ShapeDtypeStruct((bins, span_x, span_y), f32),
        in_specs=[VMEM, VMEM, smem, smem, smem, smem],
        out_specs=VMEM,
        scratch_shapes=[
            pltpu.VMEM((WSTEPS + 1, bins, span_y), f32),
            pltpu.VMEM((WSTEPS + 1, bins, span_y), f32),
            pltpu.VMEM((WSTEPS + 1, ND, span_x, span_y), f32),
            pltpu.VMEM((WSTEPS, bins, span_y), f32),
            pltpu.VMEM((WSTEPS, bins, span_y), f32),
            pltpu.VMEM((WSTEPS, ND, span_x, span_y), f32),
            pltpu.VMEM((6, span_x, span_y), f32),
            pltpu.VMEM((6, span_x, span_y), f32),
            pltpu.VMEM((6, span_x, span_y), f32),
        ]
        + sems,
        compiler_params=pltpu.CompilerParams(
            collective_id=1, has_side_effects=True, vmem_limit_bytes=48 * 1024 * 1024
        ),
    )(spectra.reshape(bins, span_x, span_y), fields, *tables)
    return result.reshape(ND, NF, span_x, span_y)


def ocean_kernel(
    zonal, meridional, height, stress, sea_in, coriolis_in, thick, inverse, mixing,
    out_z, out_m, out_h, plane, other, s_up, s_down, r_up, r_down, s_side, r_side,
):
    t, c = lax.axis_index("tile"), lax.axis_index("col")
    tiles = lax.axis_size("tile")
    levels, rows, cols = zonal.shape
    has_up, has_down = enter(t, c, tiles)
    sea = sea_in[...].astype(jnp.float32)
    coriolis = coriolis_in[...]
    own = slice(8, 8 + rows)
    wide = rows + 16
    lane = lax.broadcasted_iota(jnp.int32, (wide, cols), 1)
    line = lax.broadcasted_iota(jnp.int32, (wide, cols), 0)
    first_row = jnp.where(has_up, 0, 8)
    end_row = jnp.where(has_down, wide, 8 + rows)
    inside = jnp.where(jnp.logical_and(line >= first_row, line < end_row), 1.0, 0.0)
    is0 = jnp.where(c == 0, 1.0, 0.0)
    is1 = 1.0 - is0

    @pl.when(jnp.logical_not(has_up))
    def _():
        plane[:, :, 0:8, :] = jnp.zeros((OSTEPS, 6, 8, cols), jnp.float32)

    @pl.when(jnp.logical_not(has_down))
    def _():
        plane[:, :, 8 + rows : wide, :] = jnp.zeros((OSTEPS, 6, 8, cols), jnp.float32)

    def dx(value, beside, left, right):
        ahead = jnp.where(lane == cols - 1, pltpu.roll(beside, cols - 1, 1) * right, pltpu.roll(value, cols - 1, 1))
        back = jnp.where(lane == 0, pltpu.roll(beside, 1, 1) * left, pltpu.roll(value, 1, 1))
        return 0.5 * (ahead - back)

    def dy(value):
        return 0.5 * (pltpu.roll(value, wide - 1, 0) - pltpu.roll(value, 1, 0))

    zero = jnp.zeros((rows, cols), jnp.float32)

    def load(k, carry):
        z, m = zonal[k] * sea, meridional[k] * sea
        out_z[k] = z
        out_m[k] = m
        return carry[0] + thick[k] * z, carry[1] + thick[k] * m, carry[2] + thick[k]

    tx, ty, depth = lax.fori_loop(0, levels, load, (zero, zero, zero))
    now = height[...]
    force_x = force_y = zero
    for n in range(OSTEPS):
        plane[n, 0, own, :] = tx / depth
        plane[n, 1, own, :] = ty / depth
        plane[n, 2, own, :] = now
        count = 6 if n == 0 else 3
        if n == 0:
            for i in range(3):
                plane[n, 3 + i, own, :] = stress[i]
        part = pl.ds(0, count)
        top, bottom = pl.ds(8, 8), pl.ds(rows, 8)
        head, tail = pl.ds(0, 8), pl.ds(8 + rows, 8)
        up = remote(plane.at[n, part, top], plane.at[n, part, tail], s_up.at[n], r_down.at[n], tile=t - 1)
        up_in = remote(plane.at[n, part, top], plane.at[n, part, head], s_up.at[n], r_up.at[n], tile=t - 1)
        down = remote(plane.at[n, part, bottom], plane.at[n, part, head], s_down.at[n], r_up.at[n], tile=t + 1)
        down_in = remote(plane.at[n, part, bottom], plane.at[n, part, tail], s_down.at[n], r_down.at[n], tile=t + 1)
        pl.when(has_up)(up.start)
        pl.when(has_down)(down.start)
        pl.when(has_up)(up.wait_send)
        pl.when(has_up)(up_in.wait_recv)
        pl.when(has_down)(down.wait_send)
        pl.when(has_down)(down_in.wait_recv)
        side = remote(plane.at[n, part], other.at[n, part], s_side.at[n], r_side.at[n], col=1 - c)
        side.start()
        side.wait_send()
        side.wait_recv()
        mine = [plane[n, i] for i in range(count)]
        near = [other[n, i] for i in range(count)]
        if n == 0:
            slope = [dx(mine[3 + i], near[3 + i], is1, is0) for i in range(2)]
            force_x = (-0.5 * (slope[0] + dy(mine[4])))[own]
            force_y = (-0.5 * (slope[1] + dy(mine[5])))[own]
        high = (mine[2] - 0.2 * (dx(mine[0], near[0], is1, is0) + dy(mine[1]))) * inside
        high_near = (near[2] - 0.2 * (dx(near[0], mine[0], is0, is1) + dy(near[1]))) * inside
        press_x = (0.2 * dx(high, high_near, is1, is0))[own]
        press_y = (0.2 * dy(high))[own]
        now = high[own]

        def level(k, carry):
            tx, ty, flux_z, flux_m, z, m = carry
            z_next, m_next = out_z[k + 1], out_m[k + 1]
            low_z = mixing[k + 1] * (z - z_next)
            low_m = mixing[k + 1] * (m - m_next)
            new_z = (z + coriolis * m - press_x + (flux_z - low_z) * inverse[k]) * sea
            new_m = (m - coriolis * z - press_y + (flux_m - low_m) * inverse[k]) * sea
            out_z[k] = new_z
            out_m[k] = new_m
            return tx + thick[k] * new_z, ty + thick[k] * new_m, low_z, low_m, z_next, m_next

        def several(g, carry):
            for i in range(LEVELS):
                carry = level(g * LEVELS + i, carry)
            return carry

        carry = (zero, zero, force_x, force_y, out_z[0], out_m[0])
        groups = (levels - 1) // LEVELS
        carry = lax.fori_loop(0, groups, several, carry)
        tx, ty, flux_z, flux_m, z, m = lax.fori_loop(groups * LEVELS, levels - 1, level, carry)
        k = levels - 1
        new_z = (z + coriolis * m - press_x + (flux_z - mixing[0] * z) * inverse[k]) * sea
        new_m = (m - coriolis * z - press_y + (flux_m - mixing[0] * m) * inverse[k]) * sea
        out_z[k] = new_z
        out_m[k] = new_m
        tx, ty = tx + thick[k] * new_z, ty + thick[k] * new_m
    out_h[...] = now


def ocean_steps(zonal, meridional, height, stress, sea, coriolis, thickness, mixing):
    rows, cols = height.shape
    smem = pl.BlockSpec(memory_space=pltpu.SMEM)
    f32 = jnp.float32
    flow = jax.ShapeDtypeStruct(zonal.shape, f32)
    return pl.pallas_call(
        ocean_kernel,
        out_shape=(flow, flow, jax.ShapeDtypeStruct(height.shape, f32)),
        in_specs=[VMEM] * 6 + [smem] * 3,
        out_specs=(VMEM, VMEM, VMEM),
        scratch_shapes=[pltpu.VMEM((OSTEPS, 6, rows + 16, cols), f32)] * 2
        + [pltpu.SemaphoreType.DMA((OSTEPS,))] * 6,
        compiler_params=pltpu.CompilerParams(
            collective_id=2, has_side_effects=True, vmem_limit_bytes=32 * 1024 * 1024
        ),
    )(zonal, meridional, height, stress, sea, coriolis, thickness, 1.0 / thickness, mixing)


def body(
    zonal_velocity,
    meridional_velocity,
    surface_height,
    thickness,
    mixing,
    ocean_wet,
    spectra,
    wind_speed,
    wind_direction,
    wave_wet,
    remap_source,
    remap_target,
    remap_weight,
):
    tables = spectral_tables()
    rows, cols = surface_height.shape
    total_rows = rows * lax.axis_size("tile")
    sea_cells = ocean_wet.astype(jnp.float32)
    wet_cells = wave_wet.astype(jnp.float32)
    surface = jnp.stack(
        [zonal_velocity[0] * sea_cells, meridional_velocity[0] * sea_cells, surface_height]
    )
    currents, ocean_stress = remap(
        spectra, wave_wet, surface, remap_source, remap_target, remap_weight
    )
    fields = jnp.stack(
        [
            0.03 * currents[0],
            0.03 * currents[1],
            wet_cells,
            wind_speed * jnp.cos(wind_direction),
            wind_speed * jnp.sin(wind_direction),
            currents[2],
        ]
    )
    energy = wave_steps(spectra, fields, tables)
    row_start = lax.axis_index("tile") * rows
    coriolis = (
        0.1 + 0.1 * ((row_start + jnp.arange(rows)).astype(jnp.float32) + 0.5) / total_rows
    )[:, None] + jnp.zeros((rows, cols), jnp.float32)
    zonal, meridional, height = ocean_steps(
        zonal_velocity, meridional_velocity, surface_height, ocean_stress, ocean_wet, coriolis,
        thickness, mixing,
    )
    return (zonal, meridional, height, energy)


def solution(mesh):
    return jax.shard_map(
        body,
        mesh=mesh,
        in_specs=(
            P(None, ("groups", "tile"), "col"),
            P(None, ("groups", "tile"), "col"),
            P(("groups", "tile"), "col"),
            P(),
            P(),
            P(("groups", "tile"), "col"),
            P(None, None, ("groups", "tile"), "col"),
            P(("groups", "tile"), "col"),
            P(("groups", "tile"), "col"),
            P(("groups", "tile"), "col"),
            P(("groups", "tile", "col"), None, None),
            P(("groups", "tile", "col"), None, None),
            P(("groups", "tile", "col"), None, None),
        ),
        out_specs=(
            P(None, ("groups", "tile"), "col"),
            P(None, ("groups", "tile"), "col"),
            P(("groups", "tile"), "col"),
            P(None, None, ("groups", "tile"), "col"),
        ),
        check_vma=False,
    )
```

```python
import math

import jax
import jax.numpy as jnp
from jax import lax
from jax.experimental import pallas as pl
from jax.experimental.pallas import tpu as pltpu
from jax.sharding import PartitionSpec as P

ND = 36
NF = 32
WSTEPS = 4
OSTEPS = 4


def spectral_tables():
    angles = (jnp.arange(ND, dtype=jnp.float32) + 0.5) * (2.0 * math.pi / ND)
    group_speed = 0.5 * jnp.power(jnp.float32(1.1), -jnp.arange(NF, dtype=jnp.float32))
    freq_weight = 2.0 * (jnp.arange(NF, dtype=jnp.float32) + 1.0) / NF
    return (jnp.cos(angles), jnp.sin(angles), group_speed, freq_weight)


def split_parts(x):
    high = x.astype(jnp.bfloat16).astype(jnp.float32)
    rest = x - high
    middle = rest.astype(jnp.bfloat16).astype(jnp.float32)
    low = rest - middle
    return jnp.concatenate([high, middle, low], axis=0).astype(jnp.bfloat16)


def join_parts(r):
    return r[0:8] + r[8:16] + r[16:24]


def block_onehot(source_row, j, row_length, width):
    cells = source_row.shape[1]
    n = lax.broadcasted_iota(jnp.int32, (cells, cells), 0)
    ids = (n // width) * row_length + j * width + n % width
    return jnp.where(ids == source_row, 1.0, 0.0).astype(jnp.bfloat16)


def wave_onehot(target_row, cells):
    n = lax.broadcasted_iota(jnp.int32, (cells, target_row.shape[1]), 0)
    return jnp.where(n == target_row, 1.0, 0.0).astype(jnp.bfloat16)


NN = (((1,), (0,)), ((), ()))
NT = (((1,), (1,)), ((), ()))


def gather_kernel(row_length, width, spectra, wet, surface, source, target, weight, out, flat):
    span_x, span_y = wet.shape
    peers = source.shape[0]
    zero = jnp.zeros((span_x, span_y), jnp.float32)
    acc = [zero, zero, zero]
    for d in range(ND):
        theta = (d + 0.5) * (2.0 * math.pi / ND)
        part = jnp.sum(spectra[d], axis=0)
        cos, sin = math.cos(theta), math.sin(theta)
        for c, m in enumerate((cos * cos, cos * sin, sin * sin)):
            acc[c] = acc[c] + part * (m * 0.5 / (ND * NF))
    wetf = wet[...].astype(jnp.float32)
    flat[...] = jnp.zeros_like(flat)
    for c in range(3):
        plane = acc[c] * wetf
        for x in range(span_x):
            flat[3 + c : 4 + c, x * span_y : (x + 1) * span_y] = plane[x : x + 1, :]
    stress = split_parts(flat[...])

    def step(j, carry):
        hot = block_onehot(source[j], j, row_length, width)
        values = join_parts(
            lax.dot_general(split_parts(surface[j]), hot, NN, preferred_element_type=jnp.float32)
        )
        hot2 = wave_onehot(target[j], span_x * span_y)
        back = join_parts(
            lax.dot_general(stress, hot2, NN, preferred_element_type=jnp.float32)
        )
        out[j] = values * weight[j] + back
        return carry

    lax.fori_loop(0, peers, step, 0)


def swap_kernel(src, dst, send_sem, recv_sem, local_sem):
    peers = src.shape[0]
    t = lax.axis_index("tile")
    c = lax.axis_index("col")
    side = t // peers
    slot = lax.rem(t, peers)
    barrier = pltpu.get_barrier_semaphore()

    def partner(j):
        return {"tile": c * peers + j, "col": side}

    def copy(j):
        return pltpu.make_async_remote_copy(
            src_ref=src.at[j],
            dst_ref=dst.at[slot],
            send_sem=send_sem.at[j],
            recv_sem=recv_sem.at[slot],
            device_id=partner(j),
            device_id_type=pl.DeviceIdType.MESH,
        )

    def arrival(j):
        return pltpu.make_async_remote_copy(
            src_ref=src.at[j],
            dst_ref=dst.at[j],
            send_sem=send_sem.at[j],
            recv_sem=recv_sem.at[j],
            device_id=partner(j),
            device_id_type=pl.DeviceIdType.MESH,
        )

    def other(j):
        return jnp.logical_or(side != c, slot != j)

    for j in range(peers):

        @pl.when(other(j))
        def _():
            pl.semaphore_signal(
                barrier, inc=1, device_id=partner(j), device_id_type=pl.DeviceIdType.MESH
            )

    @pl.when(side == c)
    def _():
        pl.semaphore_wait(barrier, peers - 1)

    @pl.when(side != c)
    def _():
        pl.semaphore_wait(barrier, peers)

    for j in range(peers):

        @pl.when(other(j))
        def _():
            copy(j).start()

        @pl.when(jnp.logical_not(other(j)))
        def _():
            own = pltpu.make_async_copy(src.at[j], dst.at[j], local_sem)
            own.start()
            own.wait()

    for j in range(peers):

        @pl.when(other(j))
        def _():
            copy(j).wait_send()
            arrival(j).wait_recv()


def scatter_kernel(row_length, width, arrived, source, target, waves, ocean):
    peers = source.shape[0]
    waves[...] = jnp.zeros_like(waves)

    def step(j, carry):
        parts = split_parts(arrived[j])
        hot = block_onehot(source[j], j, row_length, width)
        ocean[j] = join_parts(
            lax.dot_general(parts, hot, NT, preferred_element_type=jnp.float32)
        )
        hot2 = wave_onehot(target[j], waves.shape[1])
        waves[...] += join_parts(
            lax.dot_general(parts, hot2, NT, preferred_element_type=jnp.float32)
        )
        return carry

    lax.fori_loop(0, peers, step, 0)


VMEM = pl.BlockSpec(memory_space=pltpu.VMEM)


def remap(spectra, wave_wet, surface, remap_source, remap_target, remap_weight):
    peers, slots = remap_source.shape[1:]
    span_x, span_y = wave_wet.shape
    rows, cols = surface.shape[1:]
    width = cols // peers
    source = remap_source.reshape(peers, 1, slots)
    target = remap_target.reshape(peers, 1, slots)
    weight = remap_weight.reshape(peers, 1, slots)
    blocks = surface.reshape(3, rows, peers, width).transpose(2, 0, 1, 3).reshape(peers, 3, slots)
    blocks = jnp.concatenate([blocks, jnp.zeros((peers, 5, slots), jnp.float32)], axis=1)
    shape = jax.ShapeDtypeStruct((peers, 8, slots), jnp.float32)
    sent = pl.pallas_call(
        lambda *refs: gather_kernel(cols, width, *refs),
        out_shape=shape,
        in_specs=[VMEM] * 6,
        out_specs=VMEM,
        scratch_shapes=[pltpu.VMEM((8, span_x * span_y), jnp.float32)],
        compiler_params=pltpu.CompilerParams(vmem_limit_bytes=32 * 1024 * 1024),
    )(spectra, wave_wet, blocks, source, target, weight)
    arrived = pl.pallas_call(
        swap_kernel,
        out_shape=shape,
        in_specs=[VMEM],
        out_specs=VMEM,
        scratch_shapes=[
            pltpu.SemaphoreType.DMA((peers,)),
            pltpu.SemaphoreType.DMA((peers,)),
            pltpu.SemaphoreType.DMA,
        ],
        compiler_params=pltpu.CompilerParams(collective_id=0, has_side_effects=True),
    )(sent)
    waves, ocean = pl.pallas_call(
        lambda *refs: scatter_kernel(cols, width, *refs),
        out_shape=(jax.ShapeDtypeStruct((8, span_x * span_y), jnp.float32), shape),
        in_specs=[VMEM] * 3,
        out_specs=(VMEM, VMEM),
        compiler_params=pltpu.CompilerParams(vmem_limit_bytes=32 * 1024 * 1024),
    )(arrived, source, target)
    currents = waves[:3].reshape(3, span_x, span_y)
    ocean_stress = (
        ocean[:, 3:6]
        .reshape(peers, 3, rows, width)
        .transpose(1, 2, 0, 3)
        .reshape(3, rows, cols)
    )
    return currents, ocean_stress


MESH = pl.DeviceIdType.MESH


def enter(t, c, tiles):
    barrier = pltpu.get_barrier_semaphore()
    has_up, has_down = t > 0, t < tiles - 1

    @pl.when(has_up)
    def _():
        pl.semaphore_signal(barrier, inc=1, device_id={"tile": t - 1}, device_id_type=MESH)

    @pl.when(has_down)
    def _():
        pl.semaphore_signal(barrier, inc=1, device_id={"tile": t + 1}, device_id_type=MESH)

    pl.semaphore_signal(barrier, inc=1, device_id={"col": 1 - c}, device_id_type=MESH)

    @pl.when(jnp.logical_and(has_up, has_down))
    def _():
        pl.semaphore_wait(barrier, 3)

    @pl.when(jnp.logical_not(jnp.logical_and(has_up, has_down)))
    def _():
        pl.semaphore_wait(barrier, 2)

    return has_up, has_down


def remote(src, dst, send, recv, **where):
    return pltpu.make_async_remote_copy(
        src_ref=src, dst_ref=dst, send_sem=send, recv_sem=recv, device_id=where, device_id_type=MESH
    )


CHUNKS = 4
UNROLL = 32
LEVELS = 7


def wave_kernel(
    beside_work, spectra, fields, cosd, sind, speed, freq, out,
    first, last, packed, before, after, beside, f_up, f_down, f_side,
    s_first, s_last, s_pack, r_before, r_after, r_beside, s_field, r_field,
):
    t, c = lax.axis_index("tile"), lax.axis_index("col")
    tiles = lax.axis_size("tile")
    has_up, has_down = enter(t, c, tiles)
    per_chunk = ND // CHUNKS
    chunk_rows = per_chunk * NF
    lane = lax.broadcasted_iota(jnp.int32, (8, 128), 1)
    sub = lax.broadcasted_iota(jnp.int32, (8, 128), 0)
    edge = jnp.where(c == 0, 127, 0)
    is0 = jnp.where(c == 0, 1.0, 0.0)
    is1 = 1.0 - is0

    def field_copies():
        return (
            (has_up, remote(fields, f_down, s_field.at[0], r_field.at[1], tile=t - 1),
             remote(fields, f_up, s_field.at[0], r_field.at[0], tile=t - 1)),
            (has_down, remote(fields, f_up, s_field.at[1], r_field.at[0], tile=t + 1),
             remote(fields, f_down, s_field.at[1], r_field.at[1], tile=t + 1)),
            (None, remote(fields, f_side, s_field.at[2], r_field.at[2], col=1 - c), None),
        )

    def edge_copies(n, q):
        rows = pl.ds(pl.multiple_of(q * chunk_rows, 8), chunk_rows)
        dirs = pl.ds(q * per_chunk, per_chunk)
        up = remote(first.at[n, rows], after.at[n, rows], s_first.at[n, q], r_after.at[n, q], tile=t - 1)
        up_in = remote(first.at[n, rows], before.at[n, rows], s_first.at[n, q], r_before.at[n, q], tile=t - 1)
        down = remote(last.at[n, rows], before.at[n, rows], s_last.at[n, q], r_before.at[n, q], tile=t + 1)
        down_in = remote(last.at[n, rows], after.at[n, rows], s_last.at[n, q], r_after.at[n, q], tile=t + 1)
        side = remote(packed.at[n, dirs], beside.at[n, dirs], s_pack.at[n, q], r_beside.at[n, q], col=1 - c)
        return (has_up, up, up_in), (has_down, down, down_in), (None, side, None)

    def start_all(copies):
        for cond, out_copy, in_copy in copies:
            if cond is None:
                out_copy.start()
            else:
                pl.when(cond)(out_copy.start)

    def wait_all(copies):
        for cond, out_copy, in_copy in copies:
            if cond is None:
                out_copy.wait_send()
                out_copy.wait_recv()
            else:
                pl.when(cond)(out_copy.wait_send)
                pl.when(cond)(in_copy.wait_recv)

    start_all(field_copies())

    @pl.when(jnp.logical_not(has_up))
    def _():
        before[...] = jnp.zeros_like(before)
        f_up[...] = jnp.zeros_like(f_up)

    @pl.when(jnp.logical_not(has_down))
    def _():
        after[...] = jnp.zeros_like(after)
        f_down[...] = jnp.zeros_like(f_down)

    drift_x, drift_y, wet = fields[0], fields[1], fields[2]
    wind_x, wind_y, level = fields[3], fields[4], fields[5]
    calm = 0.3 * jnp.exp(-0.5 * level) * (1.0 / (ND * NF))

    def keep_edges(n, d, base, i, f, value, pack):
        first[n, pl.ds(base + i, 1), :] = value[0:1, :]
        last[n, pl.ds(base + i, 1), :] = value[7:8, :]
        shift = lax.rem(f + 256 - edge, 128)
        return jnp.where(lane == f, pltpu.roll(value, shift, 1), pack)

    def opening(q, total):
        def one(dd, total):
            d = q * per_chunk + dd

            def group(fg, carry):
                total, pack = carry
                base = pl.multiple_of(d * NF + fg * UNROLL, UNROLL)
                for i in range(UNROLL):
                    value = spectra[base + i] * wet
                    out[base + i] = value
                    total = total + value
                    pack = keep_edges(0, d, base, i, fg * UNROLL + i, value, pack)
                return total, pack

            total, pack = lax.fori_loop(
                0, NF // UNROLL, group, (total, jnp.zeros((8, 128), jnp.float32))
            )
            packed[0, d] = pack
            return total

        total = lax.fori_loop(0, per_chunk, one, total)
        start_all(edge_copies(0, q))
        return total

    total = lax.fori_loop(0, CHUNKS, opening, jnp.zeros((8, 128), jnp.float32))
    beside_work()
    wait_all(field_copies())

    def row_before(i):
        return jnp.where(sub == 0, f_up[i][7:8], pltpu.roll(fields[i], 1, 0))

    def row_after(i):
        return jnp.where(sub == 7, f_down[i][0:1], pltpu.roll(fields[i], 7, 0))

    def lane_before(i):
        return jnp.where(lane == 0, pltpu.roll(f_side[i], 1, 1) * is1, pltpu.roll(fields[i], 1, 1))

    def lane_after(i):
        return jnp.where(
            lane == 127, pltpu.roll(f_side[i], 127, 1) * is0, pltpu.roll(fields[i], 127, 1)
        )

    faces = []
    for get, i in ((row_before, 0), (row_after, 0), (lane_before, 1), (lane_after, 1)):
        door = wet * get(2)
        faces.append((door, door * 0.5 * (fields[i] + get(i))))
    low_mask = jnp.logical_and(lane == 0, c == 1)
    high_mask = jnp.logical_and(lane == 127, c == 0)

    def column(i):
        return jnp.sum(
            jnp.where(lane == 127 - edge, f_side[i], 0.0), axis=1, keepdims=True
        ) + jnp.zeros((8, 128), jnp.float32)

    side_x, side_y, side_level = column(3), column(4), column(5)
    side_calm = 0.3 * jnp.exp(-0.5 * side_level) * (1.0 / (ND * NF))
    lane_freq = jnp.where(lane < NF, (lane + 1).astype(jnp.float32) * (2.0 / NF), 0.0)
    freq_column = (
        lax.broadcasted_iota(jnp.int32, (NF, 128), 0) + 1
    ).astype(jnp.float32) * (2.0 / NF)
    rows_of = (
        (before, f_up[3][7:8], f_up[4][7:8], 0.3 * jnp.exp(-0.5 * f_up[5][7:8]) * (1.0 / (ND * NF))),
        (after, f_down[3][0:1], f_down[4][0:1], 0.3 * jnp.exp(-0.5 * f_down[5][0:1]) * (1.0 / (ND * NF))),
    )

    def step(n, total):
        def arrive(q, carry):
            wait_all(edge_copies(n, q))
            return carry

        lax.fori_loop(0, CHUNKS, arrive, 0)

        def add(d, carry):
            rows = pl.ds(pl.multiple_of(d * NF, NF), NF)
            return carry[0] + before[n, rows], carry[1] + after[n, rows], carry[2] + beside[n, d]

        zero = jnp.zeros((NF, 128), jnp.float32)
        sums = lax.fori_loop(0, ND, add, (zero, zero, jnp.zeros((8, 128), jnp.float32)))
        fades = [jnp.sum(sums[i], axis=0, keepdims=True) * rows_of[i][3] for i in range(2)]
        side_fade = jnp.sum(sums[2], axis=1, keepdims=True) * side_calm
        fade = total * calm

        def one(d, total):
            cos, sin = cosd[d], sind[d]
            rows = pl.ds(pl.multiple_of(d * NF, NF), NF)
            for i in range(2):
                ref, wx, wy, _ = rows_of[i]
                push = 0.02 * jnp.maximum(wx * cos + wy * sin, 0.0)
                ref[n, rows] = ref[n, rows] * jnp.exp(push * freq_column - fades[i])
            push = 0.02 * jnp.maximum(side_x * cos + side_y * sin, 0.0)
            side = beside[n, d] * jnp.exp(push * lane_freq - side_fade)
            push = 0.02 * jnp.maximum(wind_x * cos + wind_y * sin, 0.0)

            def group(fg, carry):
                total, pack = carry
                base = pl.multiple_of(d * NF + fg * UNROLL, UNROLL)
                up8 = before[n, pl.ds(base, UNROLL)]
                down8 = after[n, pl.ds(base, UNROLL)]
                for i in range(UNROLL):
                    f = fg * UNROLL + i
                    e = out[base + i] * jnp.exp(push * freq[f] - fade)
                    vx, vy = speed[f] * cos, speed[f] * sin
                    halo = pltpu.roll(side, lax.rem(edge + 128 - f, 128), 1)
                    x0 = jnp.where(sub == 0, up8[i : i + 1], pltpu.roll(e, 1, 0))
                    x1 = jnp.where(sub == 7, down8[i : i + 1], pltpu.roll(e, 7, 0))
                    y0 = jnp.where(low_mask, halo, pltpu.roll(e, 1, 1))
                    y1 = jnp.where(high_mask, halo, pltpu.roll(e, 127, 1))
                    wx0 = vx * faces[0][0] + faces[0][1]
                    wx1 = vx * faces[1][0] + faces[1][1]
                    wy0 = vy * faces[2][0] + faces[2][1]
                    wy1 = vy * faces[3][0] + faces[3][1]
                    fx1 = jnp.maximum(wx1, 0.0) * e + jnp.minimum(wx1, 0.0) * x1
                    fx0 = jnp.maximum(wx0, 0.0) * x0 + jnp.minimum(wx0, 0.0) * e
                    fy1 = jnp.maximum(wy1, 0.0) * e + jnp.minimum(wy1, 0.0) * y1
                    fy0 = jnp.maximum(wy0, 0.0) * y0 + jnp.minimum(wy0, 0.0) * e
                    value = e - (fx1 - fx0) - (fy1 - fy0)
                    out[base + i] = value
                    total = total + value
                    pack = keep_edges(n + 1, d, base, i, f, value, pack)
                return total, pack

            total, pack = lax.fori_loop(
                0, NF // UNROLL, group, (total, jnp.zeros((8, 128), jnp.float32))
            )
            packed[n + 1, d] = pack
            return total

        def chunk(q, total):
            total = lax.fori_loop(q * per_chunk, (q + 1) * per_chunk, one, total)

            @pl.when(n < WSTEPS - 1)
            def _():
                start_all(edge_copies(n + 1, q))

            return total

        return lax.fori_loop(0, CHUNKS, chunk, jnp.zeros((8, 128), jnp.float32))

    lax.fori_loop(0, WSTEPS, step, total)


def ocean_kernel(
    zonal, meridional, height, stress, sea_in, coriolis_in, thick, inverse, mixing,
    out_z, out_m, out_h, plane, other, s_up, s_down, r_up, r_down, s_side, r_side,
):
    t, c = lax.axis_index("tile"), lax.axis_index("col")
    tiles = lax.axis_size("tile")
    levels, rows, cols = zonal.shape
    has_up, has_down = t > 0, t < tiles - 1
    sea = sea_in[...].astype(jnp.float32)
    coriolis = coriolis_in[...]
    own = slice(8, 8 + rows)
    wide = rows + 16
    lane = lax.broadcasted_iota(jnp.int32, (wide, cols), 1)
    line = lax.broadcasted_iota(jnp.int32, (wide, cols), 0)
    first_row = jnp.where(has_up, 0, 8)
    end_row = jnp.where(has_down, wide, 8 + rows)
    inside = jnp.where(jnp.logical_and(line >= first_row, line < end_row), 1.0, 0.0)
    is0 = jnp.where(c == 0, 1.0, 0.0)
    is1 = 1.0 - is0

    @pl.when(jnp.logical_not(has_up))
    def _():
        plane[:, :, 0:8, :] = jnp.zeros((OSTEPS, 6, 8, cols), jnp.float32)

    @pl.when(jnp.logical_not(has_down))
    def _():
        plane[:, :, 8 + rows : wide, :] = jnp.zeros((OSTEPS, 6, 8, cols), jnp.float32)

    def dx(value, beside, left, right):
        ahead = jnp.where(lane == cols - 1, pltpu.roll(beside, cols - 1, 1) * right, pltpu.roll(value, cols - 1, 1))
        back = jnp.where(lane == 0, pltpu.roll(beside, 1, 1) * left, pltpu.roll(value, 1, 1))
        return 0.5 * (ahead - back)

    def dy(value):
        return 0.5 * (pltpu.roll(value, wide - 1, 0) - pltpu.roll(value, 1, 0))

    zero = jnp.zeros((rows, cols), jnp.float32)

    def load(k, carry):
        z, m = zonal[k] * sea, meridional[k] * sea
        out_z[k] = z
        out_m[k] = m
        return carry[0] + thick[k] * z, carry[1] + thick[k] * m, carry[2] + thick[k]

    tx, ty, depth = lax.fori_loop(0, levels, load, (zero, zero, zero))
    now = height[...]
    force_x = force_y = zero
    for n in range(OSTEPS):
        plane[n, 0, own, :] = tx / depth
        plane[n, 1, own, :] = ty / depth
        plane[n, 2, own, :] = now
        count = 6 if n == 0 else 3
        if n == 0:
            for i in range(3):
                plane[n, 3 + i, own, :] = stress[i]
        part = pl.ds(0, count)
        top, bottom = pl.ds(8, 8), pl.ds(rows, 8)
        head, tail = pl.ds(0, 8), pl.ds(8 + rows, 8)
        up = remote(plane.at[n, part, top], plane.at[n, part, tail], s_up.at[n], r_down.at[n], tile=t - 1)
        up_in = remote(plane.at[n, part, top], plane.at[n, part, head], s_up.at[n], r_up.at[n], tile=t - 1)
        down = remote(plane.at[n, part, bottom], plane.at[n, part, head], s_down.at[n], r_up.at[n], tile=t + 1)
        down_in = remote(plane.at[n, part, bottom], plane.at[n, part, tail], s_down.at[n], r_down.at[n], tile=t + 1)
        pl.when(has_up)(up.start)
        pl.when(has_down)(down.start)
        pl.when(has_up)(up.wait_send)
        pl.when(has_up)(up_in.wait_recv)
        pl.when(has_down)(down.wait_send)
        pl.when(has_down)(down_in.wait_recv)
        side = remote(plane.at[n, part], other.at[n, part], s_side.at[n], r_side.at[n], col=1 - c)
        side.start()
        side.wait_send()
        side.wait_recv()
        mine = [plane[n, i] for i in range(count)]
        near = [other[n, i] for i in range(count)]
        if n == 0:
            slope = [dx(mine[3 + i], near[3 + i], is1, is0) for i in range(2)]
            force_x = (-0.5 * (slope[0] + dy(mine[4])))[own]
            force_y = (-0.5 * (slope[1] + dy(mine[5])))[own]
        high = (mine[2] - 0.2 * (dx(mine[0], near[0], is1, is0) + dy(mine[1]))) * inside
        high_near = (near[2] - 0.2 * (dx(near[0], mine[0], is0, is1) + dy(near[1]))) * inside
        press_x = (0.2 * dx(high, high_near, is1, is0))[own]
        press_y = (0.2 * dy(high))[own]
        now = high[own]

        def level(k, carry):
            tx, ty, flux_z, flux_m, z, m = carry
            z_next, m_next = out_z[k + 1], out_m[k + 1]
            low_z = mixing[k + 1] * (z - z_next)
            low_m = mixing[k + 1] * (m - m_next)
            new_z = (z + coriolis * m - press_x + (flux_z - low_z) * inverse[k]) * sea
            new_m = (m - coriolis * z - press_y + (flux_m - low_m) * inverse[k]) * sea
            out_z[k] = new_z
            out_m[k] = new_m
            return tx + thick[k] * new_z, ty + thick[k] * new_m, low_z, low_m, z_next, m_next

        def several(g, carry):
            for i in range(LEVELS):
                carry = level(g * LEVELS + i, carry)
            return carry

        carry = (zero, zero, force_x, force_y, out_z[0], out_m[0])
        groups = (levels - 1) // LEVELS
        carry = lax.fori_loop(0, groups, several, carry)
        tx, ty, flux_z, flux_m, z, m = lax.fori_loop(groups * LEVELS, levels - 1, level, carry)
        k = levels - 1
        new_z = (z + coriolis * m - press_x + (flux_z - mixing[0] * z) * inverse[k]) * sea
        new_m = (m - coriolis * z - press_y + (flux_m - mixing[0] * m) * inverse[k]) * sea
        out_z[k] = new_z
        out_m[k] = new_m
        tx, ty = tx + thick[k] * new_z, ty + thick[k] * new_m
    out_h[...] = now


def both_kernel(*refs):
    waves_in, ocean_in, wave_out, ocean_out = refs[:6], refs[6:15], refs[15], refs[16:19]
    waves_scratch, ocean_scratch = refs[19:36], refs[36:]

    def ocean():
        ocean_kernel(*ocean_in, *ocean_out, *ocean_scratch)

    wave_kernel(ocean, *waves_in, wave_out, *waves_scratch)


def both_steps(spectra, fields, tables, zonal, meridional, height, stress, sea, coriolis, thickness, mixing):
    _, _, span_x, span_y = spectra.shape
    rows, cols = height.shape
    bins = ND * NF
    smem = pl.BlockSpec(memory_space=pltpu.SMEM)
    dma = pltpu.SemaphoreType.DMA
    f32 = jnp.float32
    flow = jax.ShapeDtypeStruct(zonal.shape, f32)
    energy, new_zonal, new_meridional, new_height = pl.pallas_call(
        both_kernel,
        out_shape=(
            jax.ShapeDtypeStruct((bins, span_x, span_y), f32),
            flow,
            flow,
            jax.ShapeDtypeStruct(height.shape, f32),
        ),
        in_specs=[VMEM] * 2 + [smem] * 4 + [VMEM] * 6 + [smem] * 3,
        out_specs=(VMEM, VMEM, VMEM, VMEM),
        scratch_shapes=[
            pltpu.VMEM((WSTEPS + 1, bins, span_y), f32),
            pltpu.VMEM((WSTEPS + 1, bins, span_y), f32),
            pltpu.VMEM((WSTEPS + 1, ND, span_x, span_y), f32),
            pltpu.VMEM((WSTEPS, bins, span_y), f32),
            pltpu.VMEM((WSTEPS, bins, span_y), f32),
            pltpu.VMEM((WSTEPS, ND, span_x, span_y), f32),
            pltpu.VMEM((6, span_x, span_y), f32),
            pltpu.VMEM((6, span_x, span_y), f32),
            pltpu.VMEM((6, span_x, span_y), f32),
        ]
        + [dma((WSTEPS, CHUNKS))] * 6
        + [dma((3,))] * 2
        + [pltpu.VMEM((OSTEPS, 6, rows + 16, cols), f32)] * 2
        + [dma((OSTEPS,))] * 6,
        compiler_params=pltpu.CompilerParams(
            collective_id=1, has_side_effects=True, vmem_limit_bytes=48 * 1024 * 1024
        ),
    )(
        spectra.reshape(bins, span_x, span_y), fields, *tables,
        zonal, meridional, height, stress, sea, coriolis, thickness, 1.0 / thickness, mixing,
    )
    return new_zonal, new_meridional, new_height, energy.reshape(spectra.shape)


def body(
    zonal_velocity,
    meridional_velocity,
    surface_height,
    thickness,
    mixing,
    ocean_wet,
    spectra,
    wind_speed,
    wind_direction,
    wave_wet,
    remap_source,
    remap_target,
    remap_weight,
):
    tables = spectral_tables()
    rows, cols = surface_height.shape
    total_rows = rows * lax.axis_size("tile")
    sea_cells = ocean_wet.astype(jnp.float32)
    wet_cells = wave_wet.astype(jnp.float32)
    surface = jnp.stack(
        [zonal_velocity[0] * sea_cells, meridional_velocity[0] * sea_cells, surface_height]
    )
    currents, ocean_stress = remap(
        spectra, wave_wet, surface, remap_source, remap_target, remap_weight
    )
    fields = jnp.stack(
        [
            0.03 * currents[0],
            0.03 * currents[1],
            wet_cells,
            wind_speed * jnp.cos(wind_direction),
            wind_speed * jnp.sin(wind_direction),
            currents[2],
        ]
    )
    row_start = lax.axis_index("tile") * rows
    coriolis = (
        0.1 + 0.1 * ((row_start + jnp.arange(rows)).astype(jnp.float32) + 0.5) / total_rows
    )[:, None] + jnp.zeros((rows, cols), jnp.float32)
    return both_steps(
        spectra, fields, tables, zonal_velocity, meridional_velocity, surface_height, ocean_stress, ocean_wet, coriolis,
        thickness, mixing,
    )


def solution(mesh):
    return jax.shard_map(
        body,
        mesh=mesh,
        in_specs=(
            P(None, ("groups", "tile"), "col"),
            P(None, ("groups", "tile"), "col"),
            P(("groups", "tile"), "col"),
            P(),
            P(),
            P(("groups", "tile"), "col"),
            P(None, None, ("groups", "tile"), "col"),
            P(("groups", "tile"), "col"),
            P(("groups", "tile"), "col"),
            P(("groups", "tile"), "col"),
            P(("groups", "tile", "col"), None, None),
            P(("groups", "tile", "col"), None, None),
            P(("groups", "tile", "col"), None, None),
        ),
        out_specs=(
            P(None, ("groups", "tile"), "col"),
            P(None, ("groups", "tile"), "col"),
            P(("groups", "tile"), "col"),
            P(None, None, ("groups", "tile"), "col"),
        ),
        check_vma=False,
    )
```

```python
import math

import jax
import jax.numpy as jnp
from jax import lax
from jax.experimental import pallas as pl
from jax.experimental.pallas import tpu as pltpu
from jax.sharding import PartitionSpec as P

ND = 36
NF = 32
WSTEPS = 4
OSTEPS = 4


def spectral_tables():
    angles = (jnp.arange(ND, dtype=jnp.float32) + 0.5) * (2.0 * math.pi / ND)
    group_speed = 0.5 * jnp.power(jnp.float32(1.1), -jnp.arange(NF, dtype=jnp.float32))
    freq_weight = 2.0 * (jnp.arange(NF, dtype=jnp.float32) + 1.0) / NF
    return (jnp.cos(angles), jnp.sin(angles), group_speed, freq_weight)


def split_parts(x):
    high = x.astype(jnp.bfloat16).astype(jnp.float32)
    rest = x - high
    middle = rest.astype(jnp.bfloat16).astype(jnp.float32)
    low = rest - middle
    return jnp.concatenate([high, middle, low], axis=0).astype(jnp.bfloat16)


def join_parts(r):
    return r[0:8] + r[8:16] + r[16:24]


def block_onehot(source_row, j, row_length, width):
    cells = source_row.shape[1]
    n = lax.broadcasted_iota(jnp.int32, (cells, cells), 0)
    ids = (n // width) * row_length + j * width + n % width
    return jnp.where(ids == source_row, 1.0, 0.0).astype(jnp.bfloat16)


def wave_onehot(target_row, cells):
    n = lax.broadcasted_iota(jnp.int32, (cells, target_row.shape[1]), 0)
    return jnp.where(n == target_row, 1.0, 0.0).astype(jnp.bfloat16)


NN = (((1,), (0,)), ((), ()))
NT = (((1,), (1,)), ((), ()))


def gather_kernel(row_length, width, spectra, wet, surface, source, target, weight, out, flat):
    span_x, span_y = wet.shape
    peers = source.shape[0]
    zero = jnp.zeros((span_x, span_y), jnp.float32)
    acc = [zero, zero, zero]
    for d in range(ND):
        theta = (d + 0.5) * (2.0 * math.pi / ND)
        part = jnp.sum(spectra[d], axis=0)
        cos, sin = math.cos(theta), math.sin(theta)
        for c, m in enumerate((cos * cos, cos * sin, sin * sin)):
            acc[c] = acc[c] + part * (m * 0.5 / (ND * NF))
    wetf = wet[...].astype(jnp.float32)
    flat[...] = jnp.zeros_like(flat)
    for c in range(3):
        plane = acc[c] * wetf
        for x in range(span_x):
            flat[3 + c : 4 + c, x * span_y : (x + 1) * span_y] = plane[x : x + 1, :]
    stress = split_parts(flat[...])

    def step(j, carry):
        hot = block_onehot(source[j], j, row_length, width)
        values = join_parts(
            lax.dot_general(split_parts(surface[j]), hot, NN, preferred_element_type=jnp.float32)
        )
        hot2 = wave_onehot(target[j], span_x * span_y)
        back = join_parts(
            lax.dot_general(stress, hot2, NN, preferred_element_type=jnp.float32)
        )
        out[j] = values * weight[j] + back
        return carry

    lax.fori_loop(0, peers, step, 0)


def swap_kernel(src, dst, send_sem, recv_sem, local_sem):
    peers = src.shape[0]
    t = lax.axis_index("tile")
    c = lax.axis_index("col")
    side = t // peers
    slot = lax.rem(t, peers)
    barrier = pltpu.get_barrier_semaphore()

    def partner(j):
        return {"tile": c * peers + j, "col": side}

    def copy(j):
        return pltpu.make_async_remote_copy(
            src_ref=src.at[j],
            dst_ref=dst.at[slot],
            send_sem=send_sem.at[j],
            recv_sem=recv_sem.at[slot],
            device_id=partner(j),
            device_id_type=pl.DeviceIdType.MESH,
        )

    def arrival(j):
        return pltpu.make_async_remote_copy(
            src_ref=src.at[j],
            dst_ref=dst.at[j],
            send_sem=send_sem.at[j],
            recv_sem=recv_sem.at[j],
            device_id=partner(j),
            device_id_type=pl.DeviceIdType.MESH,
        )

    def other(j):
        return jnp.logical_or(side != c, slot != j)

    for j in range(peers):

        @pl.when(other(j))
        def _():
            pl.semaphore_signal(
                barrier, inc=1, device_id=partner(j), device_id_type=pl.DeviceIdType.MESH
            )

    @pl.when(side == c)
    def _():
        pl.semaphore_wait(barrier, peers - 1)

    @pl.when(side != c)
    def _():
        pl.semaphore_wait(barrier, peers)

    for j in range(peers):

        @pl.when(other(j))
        def _():
            copy(j).start()

        @pl.when(jnp.logical_not(other(j)))
        def _():
            own = pltpu.make_async_copy(src.at[j], dst.at[j], local_sem)
            own.start()
            own.wait()

    for j in range(peers):

        @pl.when(other(j))
        def _():
            copy(j).wait_send()
            arrival(j).wait_recv()


def scatter_kernel(row_length, width, arrived, source, target, waves, ocean):
    peers = source.shape[0]
    waves[...] = jnp.zeros_like(waves)

    def step(j, carry):
        parts = split_parts(arrived[j])
        hot = block_onehot(source[j], j, row_length, width)
        ocean[j] = join_parts(
            lax.dot_general(parts, hot, NT, preferred_element_type=jnp.float32)
        )
        hot2 = wave_onehot(target[j], waves.shape[1])
        waves[...] += join_parts(
            lax.dot_general(parts, hot2, NT, preferred_element_type=jnp.float32)
        )
        return carry

    lax.fori_loop(0, peers, step, 0)


VMEM = pl.BlockSpec(memory_space=pltpu.VMEM)


def remap(spectra, wave_wet, surface, remap_source, remap_target, remap_weight):
    peers, slots = remap_source.shape[1:]
    span_x, span_y = wave_wet.shape
    rows, cols = surface.shape[1:]
    width = cols // peers
    source = remap_source.reshape(peers, 1, slots)
    target = remap_target.reshape(peers, 1, slots)
    weight = remap_weight.reshape(peers, 1, slots)
    blocks = surface.reshape(3, rows, peers, width).transpose(2, 0, 1, 3).reshape(peers, 3, slots)
    blocks = jnp.concatenate([blocks, jnp.zeros((peers, 5, slots), jnp.float32)], axis=1)
    shape = jax.ShapeDtypeStruct((peers, 8, slots), jnp.float32)
    sent = pl.pallas_call(
        lambda *refs: gather_kernel(cols, width, *refs),
        out_shape=shape,
        in_specs=[VMEM] * 6,
        out_specs=VMEM,
        scratch_shapes=[pltpu.VMEM((8, span_x * span_y), jnp.float32)],
        compiler_params=pltpu.CompilerParams(vmem_limit_bytes=32 * 1024 * 1024),
    )(spectra, wave_wet, blocks, source, target, weight)
    arrived = pl.pallas_call(
        swap_kernel,
        out_shape=shape,
        in_specs=[VMEM],
        out_specs=VMEM,
        scratch_shapes=[
            pltpu.SemaphoreType.DMA((peers,)),
            pltpu.SemaphoreType.DMA((peers,)),
            pltpu.SemaphoreType.DMA,
        ],
        compiler_params=pltpu.CompilerParams(collective_id=0, has_side_effects=True),
    )(sent)
    waves, ocean = pl.pallas_call(
        lambda *refs: scatter_kernel(cols, width, *refs),
        out_shape=(jax.ShapeDtypeStruct((8, span_x * span_y), jnp.float32), shape),
        in_specs=[VMEM] * 3,
        out_specs=(VMEM, VMEM),
        compiler_params=pltpu.CompilerParams(vmem_limit_bytes=32 * 1024 * 1024),
    )(arrived, source, target)
    currents = waves[:3].reshape(3, span_x, span_y)
    ocean_stress = (
        ocean[:, 3:6]
        .reshape(peers, 3, rows, width)
        .transpose(1, 2, 0, 3)
        .reshape(3, rows, cols)
    )
    return currents, ocean_stress


MESH = pl.DeviceIdType.MESH


def enter(t, c, tiles):
    barrier = pltpu.get_barrier_semaphore()
    has_up, has_down = t > 0, t < tiles - 1

    @pl.when(has_up)
    def _():
        pl.semaphore_signal(barrier, inc=1, device_id={"tile": t - 1}, device_id_type=MESH)

    @pl.when(has_down)
    def _():
        pl.semaphore_signal(barrier, inc=1, device_id={"tile": t + 1}, device_id_type=MESH)

    pl.semaphore_signal(barrier, inc=1, device_id={"col": 1 - c}, device_id_type=MESH)

    @pl.when(jnp.logical_and(has_up, has_down))
    def _():
        pl.semaphore_wait(barrier, 3)

    @pl.when(jnp.logical_not(jnp.logical_and(has_up, has_down)))
    def _():
        pl.semaphore_wait(barrier, 2)

    return has_up, has_down


def remote(src, dst, send, recv, **where):
    return pltpu.make_async_remote_copy(
        src_ref=src, dst_ref=dst, send_sem=send, recv_sem=recv, device_id=where, device_id_type=MESH
    )


CHUNKS = 9
UNROLL = 32
LEVELS = 7


def wave_kernel(
    beside_work, spectra, fields, cosd, sind, speed, freq, out,
    first, last, packed, before, after, beside, f_up, f_down, f_side,
    s_first, s_last, s_pack, r_before, r_after, r_beside, s_field, r_field,
):
    t, c = lax.axis_index("tile"), lax.axis_index("col")
    tiles = lax.axis_size("tile")
    has_up, has_down = enter(t, c, tiles)
    per_chunk = ND // CHUNKS
    chunk_rows = per_chunk * NF
    lane = lax.broadcasted_iota(jnp.int32, (8, 128), 1)
    sub = lax.broadcasted_iota(jnp.int32, (8, 128), 0)
    edge = jnp.where(c == 0, 127, 0)
    is0 = jnp.where(c == 0, 1.0, 0.0)
    is1 = 1.0 - is0

    def field_copies():
        return (
            (has_up, remote(fields, f_down, s_field.at[0], r_field.at[1], tile=t - 1),
             remote(fields, f_up, s_field.at[0], r_field.at[0], tile=t - 1)),
            (has_down, remote(fields, f_up, s_field.at[1], r_field.at[0], tile=t + 1),
             remote(fields, f_down, s_field.at[1], r_field.at[1], tile=t + 1)),
            (None, remote(fields, f_side, s_field.at[2], r_field.at[2], col=1 - c), None),
        )

    def edge_copies(n, q):
        rows = pl.ds(pl.multiple_of(q * chunk_rows, 8), chunk_rows)
        dirs = pl.ds(q * per_chunk, per_chunk)
        up = remote(first.at[n, rows], after.at[n, rows], s_first.at[n, q], r_after.at[n, q], tile=t - 1)
        up_in = remote(first.at[n, rows], before.at[n, rows], s_first.at[n, q], r_before.at[n, q], tile=t - 1)
        down = remote(last.at[n, rows], before.at[n, rows], s_last.at[n, q], r_before.at[n, q], tile=t + 1)
        down_in = remote(last.at[n, rows], after.at[n, rows], s_last.at[n, q], r_after.at[n, q], tile=t + 1)
        side = remote(packed.at[n, dirs], beside.at[n, dirs], s_pack.at[n, q], r_beside.at[n, q], col=1 - c)
        return (has_up, up, up_in), (has_down, down, down_in), (None, side, None)

    def start_all(copies):
        for cond, out_copy, in_copy in copies:
            if cond is None:
                out_copy.start()
            else:
                pl.when(cond)(out_copy.start)

    def wait_all(copies):
        for cond, out_copy, in_copy in copies:
            if cond is None:
                out_copy.wait_send()
                out_copy.wait_recv()
            else:
                pl.when(cond)(out_copy.wait_send)
                pl.when(cond)(in_copy.wait_recv)

    start_all(field_copies())

    @pl.when(jnp.logical_not(has_up))
    def _():
        before[...] = jnp.zeros_like(before)
        f_up[...] = jnp.zeros_like(f_up)

    @pl.when(jnp.logical_not(has_down))
    def _():
        after[...] = jnp.zeros_like(after)
        f_down[...] = jnp.zeros_like(f_down)

    drift_x, drift_y, wet = fields[0], fields[1], fields[2]
    wind_x, wind_y, level = fields[3], fields[4], fields[5]
    calm = 0.3 * jnp.exp(-0.5 * level) * (1.0 / (ND * NF))

    def keep_edges(n, d, base, i, f, value, pack):
        first[n, pl.ds(base + i, 1), :] = value[0:1, :]
        last[n, pl.ds(base + i, 1), :] = value[7:8, :]
        shift = lax.rem(f + 256 - edge, 128)
        return jnp.where(lane == f, pltpu.roll(value, shift, 1), pack)

    def opening(q, total):
        def one(dd, total):
            d = q * per_chunk + dd

            def group(fg, carry):
                total, pack = carry
                base = pl.multiple_of(d * NF + fg * UNROLL, UNROLL)
                for i in range(UNROLL):
                    value = spectra[base + i] * wet
                    out[base + i] = value
                    total = total + value
                    pack = keep_edges(0, d, base, i, fg * UNROLL + i, value, pack)
                return total, pack

            total, pack = lax.fori_loop(
                0, NF // UNROLL, group, (total, jnp.zeros((8, 128), jnp.float32))
            )
            packed[0, d] = pack
            return total

        total = lax.fori_loop(0, per_chunk, one, total)
        start_all(edge_copies(0, q))
        return total

    total = lax.fori_loop(0, CHUNKS, opening, jnp.zeros((8, 128), jnp.float32))
    beside_work()
    wait_all(field_copies())

    def row_before(i):
        return jnp.where(sub == 0, f_up[i][7:8], pltpu.roll(fields[i], 1, 0))

    def row_after(i):
        return jnp.where(sub == 7, f_down[i][0:1], pltpu.roll(fields[i], 7, 0))

    def lane_before(i):
        return jnp.where(lane == 0, pltpu.roll(f_side[i], 1, 1) * is1, pltpu.roll(fields[i], 1, 1))

    def lane_after(i):
        return jnp.where(
            lane == 127, pltpu.roll(f_side[i], 127, 1) * is0, pltpu.roll(fields[i], 127, 1)
        )

    faces = []
    for get, i in ((row_before, 0), (row_after, 0), (lane_before, 1), (lane_after, 1)):
        door = wet * get(2)
        faces.append((door, door * 0.5 * (fields[i] + get(i))))
    low_mask = jnp.logical_and(lane == 0, c == 1)
    high_mask = jnp.logical_and(lane == 127, c == 0)

    def column(i):
        return jnp.sum(
            jnp.where(lane == 127 - edge, f_side[i], 0.0), axis=1, keepdims=True
        ) + jnp.zeros((8, 128), jnp.float32)

    side_x, side_y, side_level = column(3), column(4), column(5)
    side_calm = 0.3 * jnp.exp(-0.5 * side_level) * (1.0 / (ND * NF))
    lane_freq = jnp.where(lane < NF, (lane + 1).astype(jnp.float32) * (2.0 / NF), 0.0)
    freq_column = (
        lax.broadcasted_iota(jnp.int32, (NF, 128), 0) + 1
    ).astype(jnp.float32) * (2.0 / NF)
    rows_of = (
        (before, f_up[3][7:8], f_up[4][7:8], 0.3 * jnp.exp(-0.5 * f_up[5][7:8]) * (1.0 / (ND * NF))),
        (after, f_down[3][0:1], f_down[4][0:1], 0.3 * jnp.exp(-0.5 * f_down[5][0:1]) * (1.0 / (ND * NF))),
    )

    def step(n, total):
        def arrive(q, carry):
            wait_all(edge_copies(n, q))
            return carry

        lax.fori_loop(0, CHUNKS, arrive, 0)

        def add(d, carry):
            rows = pl.ds(pl.multiple_of(d * NF, NF), NF)
            return carry[0] + before[n, rows], carry[1] + after[n, rows], carry[2] + beside[n, d]

        zero = jnp.zeros((NF, 128), jnp.float32)
        sums = lax.fori_loop(0, ND, add, (zero, zero, jnp.zeros((8, 128), jnp.float32)))
        fades = [jnp.sum(sums[i], axis=0, keepdims=True) * rows_of[i][3] for i in range(2)]
        side_fade = jnp.sum(sums[2], axis=1, keepdims=True) * side_calm
        fade = total * calm

        def one(d, total):
            cos, sin = cosd[d], sind[d]
            rows = pl.ds(pl.multiple_of(d * NF, NF), NF)
            for i in range(2):
                ref, wx, wy, _ = rows_of[i]
                push = 0.02 * jnp.maximum(wx * cos + wy * sin, 0.0)
                ref[n, rows] = ref[n, rows] * jnp.exp(push * freq_column - fades[i])
            push = 0.02 * jnp.maximum(side_x * cos + side_y * sin, 0.0)
            side = beside[n, d] * jnp.exp(push * lane_freq - side_fade)
            push = 0.02 * jnp.maximum(wind_x * cos + wind_y * sin, 0.0)

            def group(fg, carry):
                total, pack = carry
                base = pl.multiple_of(d * NF + fg * UNROLL, UNROLL)
                up8 = before[n, pl.ds(base, UNROLL)]
                down8 = after[n, pl.ds(base, UNROLL)]
                for i in range(UNROLL):
                    f = fg * UNROLL + i
                    e = out[base + i] * jnp.exp(push * freq[f] - fade)
                    vx, vy = speed[f] * cos, speed[f] * sin
                    halo = pltpu.roll(side, lax.rem(edge + 128 - f, 128), 1)
                    x0 = jnp.where(sub == 0, up8[i : i + 1], pltpu.roll(e, 1, 0))
                    x1 = jnp.where(sub == 7, down8[i : i + 1], pltpu.roll(e, 7, 0))
                    y0 = jnp.where(low_mask, halo, pltpu.roll(e, 1, 1))
                    y1 = jnp.where(high_mask, halo, pltpu.roll(e, 127, 1))
                    wx0 = vx * faces[0][0] + faces[0][1]
                    wx1 = vx * faces[1][0] + faces[1][1]
                    wy0 = vy * faces[2][0] + faces[2][1]
                    wy1 = vy * faces[3][0] + faces[3][1]
                    fx1 = jnp.maximum(wx1, 0.0) * e + jnp.minimum(wx1, 0.0) * x1
                    fx0 = jnp.maximum(wx0, 0.0) * x0 + jnp.minimum(wx0, 0.0) * e
                    fy1 = jnp.maximum(wy1, 0.0) * e + jnp.minimum(wy1, 0.0) * y1
                    fy0 = jnp.maximum(wy0, 0.0) * y0 + jnp.minimum(wy0, 0.0) * e
                    value = e - (fx1 - fx0) - (fy1 - fy0)
                    out[base + i] = value
                    total = total + value
                    pack = keep_edges(n + 1, d, base, i, f, value, pack)
                return total, pack

            total, pack = lax.fori_loop(
                0, NF // UNROLL, group, (total, jnp.zeros((8, 128), jnp.float32))
            )
            packed[n + 1, d] = pack
            return total

        def chunk(q, total):
            total = lax.fori_loop(q * per_chunk, (q + 1) * per_chunk, one, total)

            @pl.when(n < WSTEPS - 1)
            def _():
                start_all(edge_copies(n + 1, q))

            return total

        return lax.fori_loop(0, CHUNKS, chunk, jnp.zeros((8, 128), jnp.float32))

    lax.fori_loop(0, WSTEPS, step, total)


def ocean_kernel(
    zonal, meridional, height, stress, sea_in, coriolis_in, thick, inverse, mixing,
    out_z, out_m, out_h, plane, other, s_up, s_down, r_up, r_down, s_side, r_side,
):
    t, c = lax.axis_index("tile"), lax.axis_index("col")
    tiles = lax.axis_size("tile")
    levels, rows, cols = zonal.shape
    has_up, has_down = t > 0, t < tiles - 1
    sea = sea_in[...].astype(jnp.float32)
    coriolis = coriolis_in[...]
    own = slice(8, 8 + rows)
    wide = rows + 16
    lane = lax.broadcasted_iota(jnp.int32, (wide, cols), 1)
    line = lax.broadcasted_iota(jnp.int32, (wide, cols), 0)
    first_row = jnp.where(has_up, 0, 8)
    end_row = jnp.where(has_down, wide, 8 + rows)
    inside = jnp.where(jnp.logical_and(line >= first_row, line < end_row), 1.0, 0.0)
    is0 = jnp.where(c == 0, 1.0, 0.0)
    is1 = 1.0 - is0

    @pl.when(jnp.logical_not(has_up))
    def _():
        plane[:, :, 0:8, :] = jnp.zeros((OSTEPS, 6, 8, cols), jnp.float32)

    @pl.when(jnp.logical_not(has_down))
    def _():
        plane[:, :, 8 + rows : wide, :] = jnp.zeros((OSTEPS, 6, 8, cols), jnp.float32)

    def dx(value, beside, left, right):
        ahead = jnp.where(lane == cols - 1, pltpu.roll(beside, cols - 1, 1) * right, pltpu.roll(value, cols - 1, 1))
        back = jnp.where(lane == 0, pltpu.roll(beside, 1, 1) * left, pltpu.roll(value, 1, 1))
        return 0.5 * (ahead - back)

    def dy(value):
        return 0.5 * (pltpu.roll(value, wide - 1, 0) - pltpu.roll(value, 1, 0))

    zero = jnp.zeros((rows, cols), jnp.float32)

    def load(k, carry):
        z, m = zonal[k] * sea, meridional[k] * sea
        out_z[k] = z
        out_m[k] = m
        return carry[0] + thick[k] * z, carry[1] + thick[k] * m, carry[2] + thick[k]

    tx, ty, depth = lax.fori_loop(0, levels, load, (zero, zero, zero))
    now = height[...]
    force_x = force_y = zero
    for n in range(OSTEPS):
        plane[n, 0, own, :] = tx / depth
        plane[n, 1, own, :] = ty / depth
        plane[n, 2, own, :] = now
        count = 6 if n == 0 else 3
        if n == 0:
            for i in range(3):
                plane[n, 3 + i, own, :] = stress[i]
        part = pl.ds(0, count)
        top, bottom = pl.ds(8, 8), pl.ds(rows, 8)
        head, tail = pl.ds(0, 8), pl.ds(8 + rows, 8)
        up = remote(plane.at[n, part, top], plane.at[n, part, tail], s_up.at[n], r_down.at[n], tile=t - 1)
        up_in = remote(plane.at[n, part, top], plane.at[n, part, head], s_up.at[n], r_up.at[n], tile=t - 1)
        down = remote(plane.at[n, part, bottom], plane.at[n, part, head], s_down.at[n], r_up.at[n], tile=t + 1)
        down_in = remote(plane.at[n, part, bottom], plane.at[n, part, tail], s_down.at[n], r_down.at[n], tile=t + 1)
        pl.when(has_up)(up.start)
        pl.when(has_down)(down.start)
        pl.when(has_up)(up.wait_send)
        pl.when(has_up)(up_in.wait_recv)
        pl.when(has_down)(down.wait_send)
        pl.when(has_down)(down_in.wait_recv)
        side = remote(plane.at[n, part], other.at[n, part], s_side.at[n], r_side.at[n], col=1 - c)
        side.start()
        side.wait_send()
        side.wait_recv()
        mine = [plane[n, i] for i in range(count)]
        near = [other[n, i] for i in range(count)]
        if n == 0:
            slope = [dx(mine[3 + i], near[3 + i], is1, is0) for i in range(2)]
            force_x = (-0.5 * (slope[0] + dy(mine[4])))[own]
            force_y = (-0.5 * (slope[1] + dy(mine[5])))[own]
        high = (mine[2] - 0.2 * (dx(mine[0], near[0], is1, is0) + dy(mine[1]))) * inside
        high_near = (near[2] - 0.2 * (dx(near[0], mine[0], is0, is1) + dy(near[1]))) * inside
        press_x = (0.2 * dx(high, high_near, is1, is0))[own]
        press_y = (0.2 * dy(high))[own]
        now = high[own]

        def level(k, carry):
            tx, ty, flux_z, flux_m, z, m = carry
            z_next, m_next = out_z[k + 1], out_m[k + 1]
            low_z = mixing[k + 1] * (z - z_next)
            low_m = mixing[k + 1] * (m - m_next)
            new_z = (z + coriolis * m - press_x + (flux_z - low_z) * inverse[k]) * sea
            new_m = (m - coriolis * z - press_y + (flux_m - low_m) * inverse[k]) * sea
            out_z[k] = new_z
            out_m[k] = new_m
            return tx + thick[k] * new_z, ty + thick[k] * new_m, low_z, low_m, z_next, m_next

        def several(g, carry):
            for i in range(LEVELS):
                carry = level(g * LEVELS + i, carry)
            return carry

        carry = (zero, zero, force_x, force_y, out_z[0], out_m[0])
        groups = (levels - 1) // LEVELS
        carry = lax.fori_loop(0, groups, several, carry)
        tx, ty, flux_z, flux_m, z, m = lax.fori_loop(groups * LEVELS, levels - 1, level, carry)
        k = levels - 1
        new_z = (z + coriolis * m - press_x + (flux_z - mixing[0] * z) * inverse[k]) * sea
        new_m = (m - coriolis * z - press_y + (flux_m - mixing[0] * m) * inverse[k]) * sea
        out_z[k] = new_z
        out_m[k] = new_m
        tx, ty = tx + thick[k] * new_z, ty + thick[k] * new_m
    out_h[...] = now


def both_kernel(*refs):
    waves_in, ocean_in, wave_out, ocean_out = refs[:6], refs[6:15], refs[15], refs[16:19]
    waves_scratch, ocean_scratch = refs[19:36], refs[36:]

    def ocean():
        ocean_kernel(*ocean_in, *ocean_out, *ocean_scratch)

    wave_kernel(ocean, *waves_in, wave_out, *waves_scratch)


def both_steps(spectra, fields, tables, zonal, meridional, height, stress, sea, coriolis, thickness, mixing):
    _, _, span_x, span_y = spectra.shape
    rows, cols = height.shape
    bins = ND * NF
    smem = pl.BlockSpec(memory_space=pltpu.SMEM)
    dma = pltpu.SemaphoreType.DMA
    f32 = jnp.float32
    flow = jax.ShapeDtypeStruct(zonal.shape, f32)
    energy, new_zonal, new_meridional, new_height = pl.pallas_call(
        both_kernel,
        out_shape=(
            jax.ShapeDtypeStruct((bins, span_x, span_y), f32),
            flow,
            flow,
            jax.ShapeDtypeStruct(height.shape, f32),
        ),
        in_specs=[VMEM] * 2 + [smem] * 4 + [VMEM] * 6 + [smem] * 3,
        out_specs=(VMEM, VMEM, VMEM, VMEM),
        scratch_shapes=[
            pltpu.VMEM((WSTEPS + 1, bins, span_y), f32),
            pltpu.VMEM((WSTEPS + 1, bins, span_y), f32),
            pltpu.VMEM((WSTEPS + 1, ND, span_x, span_y), f32),
            pltpu.VMEM((WSTEPS, bins, span_y), f32),
            pltpu.VMEM((WSTEPS, bins, span_y), f32),
            pltpu.VMEM((WSTEPS, ND, span_x, span_y), f32),
            pltpu.VMEM((6, span_x, span_y), f32),
            pltpu.VMEM((6, span_x, span_y), f32),
            pltpu.VMEM((6, span_x, span_y), f32),
        ]
        + [dma((WSTEPS, CHUNKS))] * 6
        + [dma((3,))] * 2
        + [pltpu.VMEM((OSTEPS, 6, rows + 16, cols), f32)] * 2
        + [dma((OSTEPS,))] * 6,
        compiler_params=pltpu.CompilerParams(
            collective_id=1, has_side_effects=True, vmem_limit_bytes=48 * 1024 * 1024
        ),
    )(
        spectra.reshape(bins, span_x, span_y), fields, *tables,
        zonal, meridional, height, stress, sea, coriolis, thickness, 1.0 / thickness, mixing,
    )
    return new_zonal, new_meridional, new_height, energy.reshape(spectra.shape)


def body(
    zonal_velocity,
    meridional_velocity,
    surface_height,
    thickness,
    mixing,
    ocean_wet,
    spectra,
    wind_speed,
    wind_direction,
    wave_wet,
    remap_source,
    remap_target,
    remap_weight,
):
    tables = spectral_tables()
    rows, cols = surface_height.shape
    total_rows = rows * lax.axis_size("tile")
    sea_cells = ocean_wet.astype(jnp.float32)
    wet_cells = wave_wet.astype(jnp.float32)
    surface = jnp.stack(
        [zonal_velocity[0] * sea_cells, meridional_velocity[0] * sea_cells, surface_height]
    )
    currents, ocean_stress = remap(
        spectra, wave_wet, surface, remap_source, remap_target, remap_weight
    )
    fields = jnp.stack(
        [
            0.03 * currents[0],
            0.03 * currents[1],
            wet_cells,
            wind_speed * jnp.cos(wind_direction),
            wind_speed * jnp.sin(wind_direction),
            currents[2],
        ]
    )
    row_start = lax.axis_index("tile") * rows
    coriolis = (
        0.1 + 0.1 * ((row_start + jnp.arange(rows)).astype(jnp.float32) + 0.5) / total_rows
    )[:, None] + jnp.zeros((rows, cols), jnp.float32)
    return both_steps(
        spectra, fields, tables, zonal_velocity, meridional_velocity, surface_height, ocean_stress, ocean_wet, coriolis,
        thickness, mixing,
    )


def solution(mesh):
    return jax.shard_map(
        body,
        mesh=mesh,
        in_specs=(
            P(None, ("groups", "tile"), "col"),
            P(None, ("groups", "tile"), "col"),
            P(("groups", "tile"), "col"),
            P(),
            P(),
            P(("groups", "tile"), "col"),
            P(None, None, ("groups", "tile"), "col"),
            P(("groups", "tile"), "col"),
            P(("groups", "tile"), "col"),
            P(("groups", "tile"), "col"),
            P(("groups", "tile", "col"), None, None),
            P(("groups", "tile", "col"), None, None),
            P(("groups", "tile", "col"), None, None),
        ),
        out_specs=(
            P(None, ("groups", "tile"), "col"),
            P(None, ("groups", "tile"), "col"),
            P(("groups", "tile"), "col"),
            P(None, None, ("groups", "tile"), "col"),
        ),
        check_vma=False,
    )
```
